32 devices in a mesh: pool: 2 (over x), slab: 8 (over z, y), ch: 2 (over core).
Axes of the slice: x: 2, y: 2, z: 4, core: 2. Of those that a mesh axis runs over, the one named last changes fastest.
Arguments:
- fields: bfloat16 [2, 20, 256, 224, 128], P('pool', 'ch', 'slab'), may hold values from -6 to 6
- mode_weights: bfloat16 [2, 20, 20, 64, 4096], P('pool', 'ch', None, None, 'slab'), may hold values from -1.25 to 1.25
- lin_weights: bfloat16 [2, 20, 20], P('pool', None, 'ch'), may hold values from -1.25 to 1.25
- bias: bfloat16 [2, 20], P('pool', 'ch'), may hold values from -1 to 1
- source: int32 [8, 8], P('slab'), may hold values from -1 to 7, as said below
Outputs:
- fields_out: bfloat16 [2, 20, 256, 224, 128], P('pool', 'ch', 'slab')
The draws below stay inside these ranges and needn't reach their ends.
Inputs may be any that keep to these rules, and one draw needn't show every extreme that they name: source[s, b] is -1 (block not listed) or one of s - 1, s, s + 1; each row holds at most 2 entries equal to s - 1 and at most 2 equal to s + 1, and some row holds exactly 2 of each.
All inputs are finite; a program needn't handle non-finite values.
Results may differ from the reference program's by a relative error of at most 0.0055.
Values may be sent and summed in bfloat16 or wider, within the bound.
No kernel may reach another device: no remote copies, remote signals or barrier semaphores. Data moves between devices by JAX's collectives and lax.ppermute only.
A program may use at most 320 MiB of HBM per device.

```python
import jax
import jax.numpy as jnp
from jax import lax

C = 20
NX = 256
NY = 224
NZ = 128
M = 64
NB = 8
HOP = 2
ITERS = 1
SLABS = 8
MM = 4096


def draw_source(key, part):
    base = jax.random.fold_in(key, 17)
    key_perm, key_low, key_high, key_full, key_keep = jax.random.split(base, 5)
    slab_ids = jnp.arange(SLABS, dtype=jnp.int32)[:, None]
    row_keys = jax.random.split(key_perm, SLABS)
    perms = jax.vmap(lambda single: jax.random.permutation(single, NB))(row_keys)
    ranks = jax.vmap(lambda order: jnp.zeros(NB, jnp.int32).at[order].set(jnp.arange(NB, dtype=jnp.int32)))(perms)
    lower = jax.random.randint(key_low, (SLABS, 1), 0, HOP + 1)
    upper = jax.random.randint(key_high, (SLABS, 1), 0, HOP + 1)
    full_row = jax.random.randint(key_full, (), 1, SLABS - 1)
    lower = jnp.where(slab_ids == full_row, HOP, lower)
    upper = jnp.where(slab_ids == full_row, HOP, upper)
    keeping = jax.random.randint(key_keep, (SLABS, NB), 0, 2)
    value = jnp.where(ranks < lower, slab_ids - 1, jnp.where(ranks < lower + upper, slab_ids + 1, jnp.where(keeping == 1, slab_ids, -1)))
    value = jnp.where(value >= SLABS, -1, value)
    return value.astype(jnp.int32)


def level_of(own_key, dims, shards, low, top_value):
    gain, own = 1.0, jax.random.fold_in(own_key, 6)
    for position, parts in shards:
        steps = jnp.exp(jax.random.uniform(jax.random.fold_in(own, position), (parts,), jnp.float32, low / len(shards), top_value / len(shards)))
        gain = gain * jnp.repeat(steps, dims[position] // parts).reshape([-1 if axis == position else 1 for axis in range(len(dims))])
    return gain


def centred(rng, dims, spread, limit, pieces=(), kind=jnp.bfloat16):
    level = level_of(rng, dims, pieces, -0.22, 0.18) if pieces else 1.0
    values = jax.random.normal(rng, dims, jnp.float32) * spread * level
    return jnp.minimum(jnp.maximum(values, -limit), limit).astype(kind)


def setup_inputs(seed: int = 0) -> dict:
    key_of = jax.random.split(jax.random.key(seed), 6)
    return {
        "fields": centred(key_of[0], (2, C, NX, NY, NZ), 1.0, 6.0, ((0, 2), (1, 2), (2, 8))),
        "mode_weights": centred(key_of[1], (2, C, C, M, MM), C ** -0.5, 1.25, ((0, 2), (1, 2), (4, 8))),
        "lin_weights": centred(key_of[2], (2, C, C), C ** -0.5, 1.25, ((0, 2), (2, 2))),
        "bias": jnp.clip(jax.random.uniform(key_of[3], (2, C), jnp.float32, -1.0, 1.0) * level_of(key_of[3], (2, C), ((0, 2), (1, 2)), -0.4, 0.0), -1.0, 1.0).astype(jnp.bfloat16),
        "source": draw_source(jax.random.fold_in(key_of[5], 71), 0),
    }


def tables(length, modes):
    cells = jnp.arange(length, dtype=jnp.float32)
    order = jnp.arange(modes, dtype=jnp.int32)
    half = modes // 2
    freq = jnp.where(order < half, order, order - half + 1).astype(jnp.float32)
    angle = 2.0 * jnp.pi * freq[:, None] * cells[None, :] / length
    forward = jnp.where((order < half)[:, None], jnp.cos(angle), jnp.sin(angle))
    return forward.astype(jnp.bfloat16), (forward.T * (2.0 / length)).astype(jnp.bfloat16)


def interp_table(length):
    fine_idx = jnp.arange(length, dtype=jnp.int32)[:, None]
    coarse_idx = jnp.arange(length, dtype=jnp.int32)[None, :]
    centre = length // 4 + fine_idx // 2
    second = centre - 1 + 2 * (fine_idx % 2)
    return 0.75 * (coarse_idx == centre).astype(jnp.float32) + 0.25 * (coarse_idx == second).astype(jnp.float32)


def as_float(array):
    return array.astype(jnp.float32)


def neighbour(array, offset, axis):
    length = array.shape[axis]
    zeros = jnp.zeros_like(lax.slice_in_dim(array, 0, 1, axis=axis))
    if offset == 1:
        return jnp.concatenate([lax.slice_in_dim(array, 1, length, axis=axis), zeros], axis=axis)
    return jnp.concatenate([zeros, lax.slice_in_dim(array, 0, length - 1, axis=axis)], axis=axis)


def spectral(field, weights, all_tables):
    fwd_x, inv_x, fwd_y, inv_y, fwd_z, inv_z = all_tables
    along_y = jnp.einsum('cxyz,my->cxmz', as_float(field), as_float(fwd_y)).astype(jnp.bfloat16)
    along_z = jnp.einsum('cxmz,kz->cxmk', as_float(along_y), as_float(fwd_z)).astype(jnp.bfloat16)
    along_z = along_z.reshape(C, NX, M * M)
    coeffs = jnp.einsum('cxq,nx->cnq', as_float(along_z), as_float(fwd_x)).astype(jnp.bfloat16)
    mixed = jnp.einsum('inq,ionq->onq', as_float(coeffs), as_float(weights)).astype(jnp.bfloat16)
    back_x = jnp.einsum('onq,xn->oxq', as_float(mixed), as_float(inv_x)).astype(jnp.bfloat16)
    back_x = back_x.reshape(C, NX, M, M)
    back_z = jnp.einsum('cxmk,zk->cxmz', as_float(back_x), as_float(inv_z)).astype(jnp.bfloat16)
    return jnp.einsum('cxmz,ym->cxyz', as_float(back_z), as_float(inv_y))


def reference(fields, mode_weights, lin_weights, bias, source):
    fwd_x, inv_x = tables(NX, M)
    fwd_y, inv_y = tables(NY, M)
    fwd_z, inv_z = tables(NZ, M)
    all_tables = (fwd_x, inv_x, fwd_y, inv_y, fwd_z, inv_z)
    pmat = interp_table(NZ)
    to_fine_table = pmat.T.astype(jnp.bfloat16)
    to_coarse_table = (0.5 * pmat).astype(jnp.bfloat16)
    planes = NX // SLABS
    block_rows = NY // NB
    slab_ids = jnp.arange(SLABS, dtype=jnp.int32)[:, None]
    shape_six = (C, SLABS, planes, NB, block_rows, NZ)

    def expand(mask):
        return as_float(mask)[None, :, None, :, None, None]

    current = [fields[0], fields[1]]
    for iteration in range(ITERS):
        totals = []
        specs = []
        for pool in range(2):
            spec = spectral(current[pool], mode_weights[pool], all_tables)
            linear = jnp.einsum('io,ixyz->oxyz', as_float(lin_weights[pool]), as_float(current[pool]))
            totals.append(spec + linear + as_float(bias[pool])[:, None, None, None])
            specs.append(spec)
        to_fine = jnp.dot(current[0], to_fine_table, preferred_element_type=jnp.float32).astype(jnp.bfloat16)
        to_coarse = jnp.dot(specs[1].astype(jnp.bfloat16), to_coarse_table, preferred_element_type=jnp.float32).astype(jnp.bfloat16)
        coarse_blocks = as_float(to_fine).reshape(shape_six)
        fine_blocks = as_float(to_coarse).reshape(shape_six)
        here = expand(source == slab_ids)
        fine_add = coarse_blocks * here
        coarse_add = fine_blocks * here
        for offset in (-1, 1):
            fine_add = fine_add + neighbour(coarse_blocks, offset, 1) * expand(source == slab_ids + offset)
            coarse_add = coarse_add + neighbour(fine_blocks, offset, 1) * expand(neighbour(source, offset, 0) == slab_ids)
        new_coarse = jax.nn.gelu(totals[0] + coarse_add.reshape(C, NX, NY, NZ), approximate=False).astype(jnp.bfloat16)
        new_fine = jax.nn.gelu(totals[1] + fine_add.reshape(C, NX, NY, NZ), approximate=False).astype(jnp.bfloat16)
        current = [new_coarse, new_fine]
    return jnp.stack(current)
```

```python
import functools

import jax
import jax.numpy as jnp
import ml_dtypes
import numpy as np
from jax import lax
from jax.experimental import pallas as pl
from jax.experimental.pallas import tpu as pltpu
from jax.sharding import PartitionSpec as P

HOP = 2
LANES = 128
BF = jnp.bfloat16
F32 = jnp.float32
ERF_POLY = (
    7.97884216e-01, 3.63342835e-02, -3.31299940e-05, -5.52401584e-05,
    3.96910946e-06, -1.33446410e-07, 1.80561642e-09,
)


def shifted(value, axis, steps):
    count = lax.axis_size(axis)
    leading, last = (max(0, -steps), min(count, count - steps))
    return lax.ppermute(value, axis, [(source, source + steps) for source in range(leading, last)])


def swapped(value, axis, apart):
    mask = 2**apart
    pairs = [(source, source ^ mask) for source in range(lax.axis_size(axis))]
    return lax.ppermute(value, axis, pairs)


def tables(length, modes):
    cells = jnp.arange(length, dtype=jnp.float32)
    order = jnp.arange(modes, dtype=jnp.int32)
    half = modes // 2
    freq = jnp.where(order < half, order, order - half + 1).astype(jnp.float32)
    angle = 2.0 * jnp.pi * freq[:, None] * cells[None, :] / length
    forward = jnp.where((order < half)[:, None], jnp.cos(angle), jnp.sin(angle))
    return (forward.astype(jnp.bfloat16), (forward.T * (2.0 / length)).astype(jnp.bfloat16))


def interp_table(length):
    fine_idx = jnp.arange(length, dtype=jnp.int32)[:, None]
    coarse_idx = jnp.arange(length, dtype=jnp.int32)[None, :]
    centre = length // 4 + fine_idx // 2
    second = centre - 1 + 2 * (fine_idx % 2)
    return 0.75 * (coarse_idx == centre).astype(jnp.float32) + 0.25 * (coarse_idx == second).astype(
        jnp.float32
    )


def host_interp(length):
    fine = np.arange(length)[:, None]
    coarse = np.arange(length)[None, :]
    centre = length // 4 + fine // 2
    second = centre - 1 + 2 * (fine % 2)
    return (0.75 * (coarse == centre) + 0.25 * (coarse == second)).astype(np.float32)


def host_tables(length, modes):
    cells = np.arange(length, dtype=np.float32)
    order = np.arange(modes)
    half = modes // 2
    freq = np.where(order < half, order, order - half + 1).astype(np.float32)
    angle = np.float32(2.0 * np.pi) * freq[:, None] * cells[None, :] / np.float32(length)
    forward = np.where((order < half)[:, None], np.cos(angle), np.sin(angle)).astype(np.float32)
    inverse = forward.T * np.float32(2.0 / length)
    return forward.astype(ml_dtypes.bfloat16), inverse.astype(ml_dtypes.bfloat16)


def two_of(table):
    zero = np.zeros_like(table)
    return np.block([[table, zero], [zero, table]])


def dot(left, right):
    return jnp.dot(left, right, preferred_element_type=F32)


def gelu(v):
    square = jnp.minimum(v * v, 36.0)
    poly = ERF_POLY[-1]
    for coef in ERF_POLY[-2::-1]:
        poly = poly * square + coef
    half = 0.5 * v
    return half + half * jnp.tanh(v * poly)


class Plan:
    def __init__(self, field, mode_local, own_row, slabs):
        self.ch, self.planes, self.ny, self.nz = field.shape
        self.modes, self.q = mode_local.shape[2], mode_local.shape[3]
        self.outs = mode_local.shape[1]
        self.blocks = own_row.shape[0]
        self.slabs = slabs
        self.nx = self.planes * slabs
        self.rows = self.ny // self.blocks
        self.half = (self.blocks - 2 * HOP) * self.rows
        self.hop = HOP * self.rows
        self.group = self.modes // slabs if self.modes % slabs == 0 else 0
        self.pairs = self.planes // 2
        self.mid_rows = 2 * self.pairs * self.half
        self.pack_rows = self.mid_rows + self.half
        self.edge_rows = -(-self.hop // 16) * 16
        self.nb_rows = self.pairs * 2 * self.hop + self.edge_rows
        total = self.ch // 2
        counts = [-(-total // 2), total // 2]
        self.groups = [(sum(counts[:i]), count) for i, count in enumerate(counts) if count]
        self.step = self.planes + 8 if self.planes % 16 == 0 else self.planes
        self.depth = 4 * self.modes + 8

    def chan_spec(self):
        return pl.BlockSpec((1, self.planes, self.ny, self.nz), lambda c: (c, 0, 0, 0))

    def fits(self):
        return (
            self.group >= 2
            and self.group % 2 == 0
            and self.slabs & (self.slabs - 1) == 0
            and self.nz == LANES
            and 2 * self.modes == LANES
            and self.ch % 2 == 0
            and self.outs == 2 * self.ch
            and self.planes % 16 == 0
            and 4 * self.planes <= LANES
            and self.ny % 16 == 0
            and self.blocks == 4 * HOP
            and self.half % 16 == 0
            and self.half == 2 * self.hop
            and self.hop % 8 == 0
            and self.hop <= 64
            and self.q == self.group * self.modes
        )


def listing(meta, plan):
    nb = plan.blocks
    slab = meta[3 * nb]
    one, zero = jnp.int32(1), jnp.int32(0)
    row = [meta[b] for b in range(nb)]
    left = [jnp.where((row[b] == slab - 1) & (row[b] >= 0), one, zero) for b in range(nb)]
    right = [jnp.where(row[b] == slab + 1, one, zero) for b in range(nb)]
    listed = [jnp.where(row[b] >= 0, one, zero) for b in range(nb)]
    near = [1 - left[b] - right[b] for b in range(nb)]
    total = functools.reduce(lambda a, b: a + b, near)
    place, rank_l, rank_r = [], [], []
    n_near, n_far, n_l, n_r = zero, total, zero, zero
    for b in range(nb):
        place.append(jnp.where(near[b] == 1, n_near, n_far))
        rank_l.append(n_l)
        rank_r.append(n_r)
        n_near, n_far = n_near + near[b], n_far + 1 - near[b]
        n_l, n_r = n_l + left[b], n_r + right[b]
    return dict(slab=slab, left=left, right=right, listed=listed, near=near, place=place,
                rank_l=rank_l, rank_r=rank_r)


def sends(meta, plan, which):
    nb = plan.blocks
    slab = meta[3 * nb]
    ask = [jnp.where(meta[which * nb + b] == slab, jnp.int32(1), jnp.int32(0)) for b in range(nb)]
    rank, count = [], jnp.int32(0)
    for b in range(nb):
        rank.append(jnp.where(ask[b] == 1, count, jnp.int32(-1)))
        count = count + ask[b]
    return rank


def steps_of(index, size, count):
    out = jnp.zeros_like(index)
    for k in range(1, count):
        out = out + jnp.where(index >= k * size, jnp.int32(1), jnp.int32(0))
    return out


def by_block(block, values):
    out = jnp.full_like(block, -1)
    for b, value in enumerate(values):
        out = jnp.where(block == b, value, out)
    return out


def chosen(mask):
    return jnp.where(mask, 1.0, 0.0).astype(F32)


def row_col(rows, cols):
    shape = (rows, cols)
    return lax.broadcasted_iota(jnp.int32, shape, 0), lax.broadcasted_iota(jnp.int32, shape, 1)


def forward_kernel(plan, fy, fz2, u, out, scr):
    planes, modes, step = plan.planes, plan.modes, plan.step
    for xp in range(plan.pairs):
        both = jnp.concatenate([u[0, 2 * xp], u[0, 2 * xp + 1]], axis=1)
        along = dot(fy[...], both)
        for side in range(2):
            scr[pl.ds(2 * xp + side, modes, stride=step), :] = along[
                :, side * LANES:(side + 1) * LANES
            ]
    for d in range(plan.slabs):
        lefts = []
        for jp in range(plan.group // 2):
            start = (d * plan.group + 2 * jp) * step
            lefts.append(jnp.concatenate(
                [scr[start:start + planes], scr[start + step:start + step + planes]], axis=1
            ))
        done = dot(jnp.concatenate(lefts, axis=0).astype(BF), fz2[...]).astype(BF)
        for jp in range(plan.group // 2):
            out[d, 0, :, jp * LANES:(jp + 1) * LANES] = done[jp * planes:(jp + 1) * planes]


def pack(plan, sel, esel, u, store, store_edges):
    lo, mid = plan.nz // 4, plan.nz // 2
    edges = jnp.zeros((plan.ny, LANES), F32)
    for c2 in range(2):
        for double in range(plan.pairs // 2):
            mids = []
            for i in range(2):
                x = 4 * double + 2 * i
                mids += [u[c2, x, :, lo:lo + mid], u[c2, x + 1, :, lo:lo + mid]]
            packed = dot(sel[...], jnp.concatenate(mids, axis=1))
            store(c2, double, [packed[:, :LANES], packed[:, LANES:]])
        for xp in range(plan.pairs):
            both = jnp.concatenate([u[c2, 2 * xp], u[c2, 2 * xp + 1]], axis=1)
            edges = edges + dot(both, esel[c2 * plan.pairs + xp])
    store_edges(dot(sel[...], edges.astype(BF)).astype(BF))


def picks(plan, info, first):
    nb = plan.blocks
    row, col = row_col(plan.half, plan.ny)
    block = steps_of(col, plan.rows, nb)
    slot = steps_of(row, plan.rows, 2 * HOP) + first
    same = row - (slot - first) * plan.rows == col - block * plan.rows
    near = by_block(block, info["near"]) == 1
    return chosen(same & near & (by_block(block, info["place"]) == slot)).astype(BF)


def pack_first_kernel(plan, meta, esel, u, h1, sel):
    half = plan.half

    @pl.when(pl.program_id(0) == 0)
    def _():
        sel[...] = picks(plan, listing(meta, plan), 0)

    def store(c2, double, tiles):
        for i, tile in enumerate(tiles):
            at = (c2 * plan.pairs + 2 * double + i) * half
            h1[0, at:at + half, :] = tile.astype(BF)

    def store_edges(packed):
        h1[0, plan.mid_rows:] = packed

    pack(plan, sel, esel, u, store, store_edges)


def pack_rest_kernel(plan, meta, esel, u, h2, right, left, sel):
    half, hop, nb = plan.half, plan.hop, plan.blocks
    pad = plan.edge_rows

    @pl.when(pl.program_id(0) == 0)
    def _():
        sel[0:half] = picks(plan, listing(meta, plan), nb - 2 * HOP)
        row, col = row_col(pad, plan.ny)
        block = steps_of(col, plan.rows, nb)
        slot = steps_of(row, plan.rows, HOP + 1)
        same = (row - slot * plan.rows == col - block * plan.rows) & (slot < HOP)
        for which in range(2):
            rank = by_block(block, sends(meta, plan, 2 - which))
            start = half + which * pad
            sel[start:start + pad] = chosen(same & (rank == slot)).astype(BF)

    def store(c2, double, tiles):
        for i, tile in enumerate(tiles):
            at = (c2 * plan.pairs + 2 * double + i) * half
            h2[0, at:at + half, :] = tile[0:half].astype(BF)
        at = (c2 * plan.pairs // 2 + double) * 2 * hop
        for ref, start in ((right, half), (left, half + pad)):
            ref[0, at:at + 2 * hop, :] = jnp.concatenate(
                [tile[start:start + hop] for tile in tiles], axis=0
            ).astype(BF)

    def store_edges(packed):
        h2[0, plan.mid_rows:] = packed[0:half]
        right[0, 2 * plan.pairs * hop:] = packed[half:half + pad]
        left[0, 2 * plan.pairs * hop:] = packed[half + pad:half + 2 * pad]

    pack(plan, sel, esel, u, store, store_edges)


def assemble_kernel(plan, meta, h2, from_left, from_right, out, sel, edge_sel):
    half, hop, nb = plan.half, plan.hop, plan.blocks
    pad = plan.edge_rows

    @pl.when(pl.program_id(0) == 0)
    def _():
        info = listing(meta, plan)

        def build(width, period, offset):
            row, col = row_col(half, 2 * width)
            side = steps_of(col, width, 2)
            within = col - side * width
            part = steps_of(within, period, max(1, width // period))
            inner = within - part * period
            slot = steps_of(inner, plan.rows, HOP + 1)
            target = steps_of(row, plan.rows, 2 * HOP)
            same = (row - target * plan.rows == inner - slot * plan.rows) & (part == offset)
            mask = jnp.zeros((half, 2 * width), F32)
            for b in range(nb):
                place = info["place"][b] - (nb - 2 * HOP)
                hit = same & (target == place)
                mask = mask + chosen(
                    hit & (side == 0) & (slot == info["rank_l"][b]) & (info["left"][b] == 1)
                ) + chosen(
                    hit & (side == 1) & (slot == info["rank_r"][b]) & (info["right"][b] == 1)
                )
            return mask.astype(BF)

        for offset in range(2):
            sel[offset] = build(2 * hop, hop, offset)
        edge_sel[...] = build(pad, pad, 0)

    @pl.loop(0, plan.pairs, unroll=4)
    def _(double):
        at = pl.multiple_of(double * 2 * hop, 16)
        sides = jnp.concatenate(
            [from_left[0, pl.ds(at, 2 * hop), :], from_right[0, pl.ds(at, 2 * hop), :]], axis=0
        )
        for i in range(2):
            to = pl.multiple_of((2 * double + i) * half, 16)
            own = h2[0, pl.ds(to, half), :].astype(F32)
            out[0, pl.ds(to, half), :] = (own + dot(sel[i], sides)).astype(BF)

    sides = jnp.concatenate(
        [from_left[0, 2 * plan.pairs * hop:], from_right[0, 2 * plan.pairs * hop:]], axis=0
    )
    own = h2[0, plan.mid_rows:].astype(F32)
    out[0, plan.mid_rows:] = (own + dot(edge_sel[...], sides)).astype(BF)


def linear_kernel(plan, w_own, w_far, bias, own, far, out):
    ch = plan.ch
    wide = w_own.shape[0] // ch
    for xp in range(own.shape[1] // 2):
        for g in range(plan.ny // wide):
            def tile(ref):
                sides = [
                    ref[:, 2 * xp + i, g * wide:(g + 1) * wide, :].reshape(ch * wide, LANES)
                    for i in range(2)
                ]
                return jnp.concatenate(sides, axis=1)

            total = dot(w_own[...], tile(own)) + dot(w_far[...], tile(far)) + bias[...]
            total = total.astype(BF)
            for i in range(2):
                out[:, 2 * xp + i, g * wide:(g + 1) * wide, :] = total[
                    :, i * LANES:(i + 1) * LANES
                ].reshape(ch, wide, LANES)


def mix_kernel(plan, fx, weights, pencils, out, coeffs):
    step = pl.program_id(0)
    ch, rows = plan.ch, weights.shape[2]

    @pl.when(step == 0)
    def _():
        @pl.loop(0, ch)
        def _(c):
            column = jnp.concatenate([pencils[d, c] for d in range(plan.slabs)], axis=0)
            coeffs[c] = dot(fx[...], column).astype(BF).astype(F32)

    start = pl.multiple_of(step * rows, rows)

    @pl.loop(0, plan.outs)
    def _(o):
        total = weights[0, o].astype(F32) * coeffs[0, pl.ds(start, rows), :]
        for c in range(1, ch):
            total = total + weights[c, o].astype(F32) * coeffs[c, pl.ds(start, rows), :]
        out[o] = total.astype(BF)


def sum_kernel(plan, mine, got, out):
    out[...] = (mine[...].astype(F32) + got[...].astype(F32)).astype(BF)


def back_x_kernel(plan, gx, mixed, out):
    done = dot(gx[...], mixed[0]).astype(BF)
    for k in range(plan.slabs):
        out[k, 0] = done[k * plan.planes:(k + 1) * plan.planes]


def final_kernel(plan, meta, gz2, gzp2, gx3, gy, interp, lin, h1, h2, modes0, owns, out, scr, wide,
                 place):
    nb, slabs, planes, modes, half = plan.blocks, plan.slabs, plan.planes, plan.modes, plan.half
    depth = plan.depth
    coarse = meta[3 * nb + 1] == 0
    step = pl.program_id(0)

    @pl.when(step == 0)
    def _():
        info = listing(meta, plan)
        row, col = row_col(plan.ny, modes)
        block = steps_of(row, plan.rows, nb)
        wide[:, 0:modes] = gy[...]
        for which, base in ((1, 1), (2, 0), (3, 2)):
            fed = by_block(block, [meta[base * nb + b] for b in range(nb)]) == info["slab"]
            wide[:, which * modes:(which + 1) * modes] = jnp.where(
                fed, gy[...].astype(F32), 0.0
            ).astype(BF)
        row, col = row_col(plan.ny, plan.ny)
        block = steps_of(row, plan.rows, nb)
        slot = steps_of(col, plan.rows, nb)
        same = row - block * plan.rows == col - slot * plan.rows
        listed = by_block(block, info["listed"]) == 1
        place[...] = chosen(same & listed & (by_block(block, info["place"]) == slot)).astype(BF)

    for d in range(slabs):
        left = jnp.concatenate(
            [owns[d, 0, :, jp * LANES:(jp + 1) * LANES] for jp in range(plan.group // 2)], axis=0
        )
        done = dot(left, gz2[...])
        for jp in range(plan.group // 2):
            for i in range(2):
                m = d * plan.group + 2 * jp + i
                scr[pl.ds(m, planes, stride=depth), :] = done[
                    jp * planes:(jp + 1) * planes, i * LANES:(i + 1) * LANES
                ]

    @pl.when(coarse)
    def _():
        for d in range(slabs):
            beside = dot(gx3[...], modes0[d, 0]).astype(BF)
            left = jnp.concatenate(
                [beside[:, jp * LANES:(jp + 1) * LANES] for jp in range(plan.group // 2)], axis=0
            )
            done = dot(left, gzp2[...])
            for jp in range(plan.group // 2):
                for which in range(3):
                    at = (jp * 3 + which) * planes
                    for i in range(2):
                        m = (which + 1) * modes + d * plan.group + 2 * jp + i
                        scr[pl.ds(m, planes, stride=depth), :] = done[
                            at:at + planes, i * LANES:(i + 1) * LANES
                        ]

    def emit(xp, total):
        for i in range(2):
            for r in range(0, plan.ny, 16):
                v = total[r:r + 16, i * LANES:(i + 1) * LANES] + lin[
                    0, 2 * xp + i, r:r + 16, :
                ].astype(F32)
                out[0, 2 * xp + i, r:r + 16, :] = gelu(v).astype(BF)

    def spread(xp, count):
        sides = []
        for i in range(2):
            at = pl.multiple_of((2 * xp + i) * depth, 8)
            sides.append(scr[pl.ds(at, count), :])
        return jnp.concatenate(sides, axis=1).astype(BF)

    @pl.when(coarse)
    def _():
        @pl.loop(0, plan.pairs, unroll=2)
        def _(xp):
            emit(xp, dot(wide[...], spread(xp, 4 * modes)))

    @pl.when(jnp.logical_not(coarse))
    def _():
        c2 = lax.rem(step, 2)

        @pl.loop(0, plan.pairs, unroll=2)
        def _(xp):
            at = pl.multiple_of((c2 * plan.pairs + xp) * half, 16)
            table = interp[c2 * plan.pairs + xp]
            parts = []
            for ref in (h1, h2):
                packed = jnp.concatenate(
                    [ref[0, pl.ds(at, half), :], ref[0, plan.mid_rows:]], axis=1
                )
                parts.append(dot(packed, table).astype(BF))
            fed = dot(place[...], jnp.concatenate(parts, axis=0))
            emit(xp, fed + dot(gy[...], spread(xp, modes)))


def whole(shape):
    return pl.BlockSpec(shape, lambda *_: (0,) * len(shape))


SCALARS = pl.BlockSpec(memory_space=pltpu.SMEM)


def edge_select(plan):
    lo, mid = plan.nz // 4, plan.nz // 2
    sel = np.zeros((2, plan.planes, plan.nz, LANES), np.float32)
    for c2 in range(2):
        for x in range(plan.planes):
            at = c2 * 2 * plan.planes + 2 * x
            sel[c2, x, lo - 1, at] = 1.0
            sel[c2, x, lo + mid, at + 1] = 1.0
    return sel


def call(kernel, plan, grid, in_specs, out_specs, out_shape, scratch, cost, args, after=(),
         onto=None):
    count = len(args)
    aliases = {}
    if onto is not None:
        aliases = {count: 0}
        after = (onto,) + tuple(after)

    def run(*refs):
        kernel(plan, *refs[:count], *refs[count + len(after):])

    flops, traffic, special = cost
    return pl.pallas_call(
        run,
        grid=grid,
        in_specs=in_specs + [pl.BlockSpec(memory_space=pl.ANY)] * len(after),
        out_specs=out_specs,
        out_shape=out_shape,
        scratch_shapes=scratch,
        input_output_aliases=aliases,
        compiler_params=pltpu.CompilerParams(vmem_limit_bytes=56 * 2**20),
        cost_estimate=pl.CostEstimate(
            flops=1000, bytes_accessed=1000, transcendentals=0
        ),
    )(*args, *after)


def gate(value, after):
    anywhere = pl.BlockSpec(memory_space=pl.ANY)
    return pl.pallas_call(
        lambda *refs: None,
        in_specs=[anywhere] * (1 + len(after)),
        out_specs=anywhere,
        out_shape=jax.ShapeDtypeStruct(value.shape, value.dtype),
        input_output_aliases={0: 0},
    )(value, *after)


def run_forward(plan, fy, fz2, field, after=()):
    shape = (plan.slabs, plan.ch, plan.planes, plan.q)
    return call(
        forward_kernel, plan, (plan.ch,),
        [whole(fy.shape), whole(fz2.shape), plan.chan_spec()],
        pl.BlockSpec((plan.slabs, 1, plan.planes, plan.q), lambda c: (0, c, 0, 0)),
        jax.ShapeDtypeStruct(shape, BF),
        [pltpu.VMEM((plan.modes * plan.step, LANES), F32)],
        (10**9, field.size * 2, 0), (fy, fz2, field), after,
    )


def run_pack(plan, meta, esel, field, group, near, after=()):
    start, count = group
    full = jax.ShapeDtypeStruct((count, plan.pack_rows, LANES), BF)
    part = jax.ShapeDtypeStruct((count, plan.nb_rows, LANES), BF)
    shapes = [full, part, part] if near else [full]
    rows = plan.half + 2 * plan.edge_rows if near else plan.half
    return call(
        pack_rest_kernel if near else pack_first_kernel, plan, (count,),
        [SCALARS, whole(esel.shape),
         pl.BlockSpec((2,) + field.shape[1:], lambda c: (c + start, 0, 0, 0))],
        [pl.BlockSpec((1,) + shape.shape[1:], lambda c: (c, 0, 0)) for shape in shapes], shapes,
        [pltpu.VMEM((rows, plan.ny), BF)],
        (10**9, field.size * 3, 0), (meta, esel, field), after,
    )


def run_assemble(plan, meta, second, from_left, from_right, after=()):
    pack_spec = pl.BlockSpec((1, plan.pack_rows, LANES), lambda c: (c, 0, 0))
    near_spec = pl.BlockSpec((1, plan.nb_rows, LANES), lambda c: (c, 0, 0))
    return call(
        assemble_kernel, plan, (second.shape[0],),
        [SCALARS, pack_spec, near_spec, near_spec], pack_spec,
        jax.ShapeDtypeStruct(second.shape, BF),
        [pltpu.VMEM((2, plan.half, 4 * plan.hop), BF),
         pltpu.VMEM((plan.half, 2 * plan.edge_rows), BF)],
        (10**9, second.size * 6, 0), (meta, second, from_left, from_right), after,
    )


def run_linear(plan, w_own, w_far, bias_rows, field, far_field, after=()):
    per = 4
    spec = pl.BlockSpec((plan.ch, per) + field.shape[2:], lambda x: (0, x, 0, 0))
    return call(
        linear_kernel, plan, (plan.planes // per,),
        [whole(w_own.shape), whole(w_far.shape), whole(bias_rows.shape), spec, spec],
        spec, jax.ShapeDtypeStruct(field.shape, BF), [],
        (2 * 10**10, field.size * 6, 0), (w_own, w_far, bias_rows, field, far_field), after,
    )


def run_mix(plan, fx, weights, pencils, after=()):
    rows = 16
    return call(
        mix_kernel, plan, (plan.modes // rows,),
        [whole(fx.shape),
         pl.BlockSpec((plan.ch, plan.outs, rows, plan.q), lambda n: (0, 0, n, 0)),
         whole(pencils.shape)],
        pl.BlockSpec((plan.outs, rows, plan.q), lambda n: (0, n, 0)),
        jax.ShapeDtypeStruct((plan.outs, plan.modes, plan.q), BF),
        [pltpu.VMEM((plan.ch, plan.modes, plan.q), F32)],
        (10**9, weights.size * 2, 0), (fx, weights, pencils), after,
    )


def run_sum(plan, mine, got, after=()):
    return call(
        sum_kernel, plan, (1,), [whole(mine.shape), whole(mine.shape)], whole(mine.shape),
        jax.ShapeDtypeStruct(mine.shape, BF), [], (1, 1, 0), (mine, got), after,
    )


def run_back_x(plan, gx, mixed, after=()):
    return call(
        back_x_kernel, plan, (plan.ch,),
        [whole(gx.shape), pl.BlockSpec((1, plan.modes, plan.q), lambda c: (c, 0, 0))],
        pl.BlockSpec((plan.slabs, 1, plan.planes, plan.q), lambda c: (0, c, 0, 0)),
        jax.ShapeDtypeStruct((plan.slabs, plan.ch, plan.planes, plan.q), BF), [],
        (10**9, mixed.size * 10, 0), (gx, mixed), after,
    )


def run_final(plan, meta, gz2, gzp2, gx3, gy, interp, lin, first, second, fine_modes, owned, group,
              onto=None, after=()):
    start, count = group
    at = 2 * start
    chan_spec = pl.BlockSpec((1,) + lin.shape[1:], lambda c: (c + at, 0, 0, 0))
    pair_spec = pl.BlockSpec((1, plan.pack_rows, LANES), lambda c: (c // 2, 0, 0))
    return call(
        final_kernel, plan, (2 * count,),
        [SCALARS, whole(gz2.shape), whole(gzp2.shape), whole(gx3.shape), whole(gy.shape),
         whole(interp.shape), chan_spec, pair_spec, pair_spec,
         pl.BlockSpec((plan.slabs, 1, plan.modes, plan.q), lambda c: (0, c, 0, 0)),
         pl.BlockSpec((plan.slabs, 1, plan.planes, plan.q), lambda c: (0, c + at, 0, 0))],
        chan_spec, jax.ShapeDtypeStruct(lin.shape, BF),
        [pltpu.VMEM((plan.planes * plan.depth, LANES), F32),
         pltpu.VMEM((plan.ny, 4 * plan.modes), BF),
         pltpu.VMEM((plan.ny, plan.ny), BF)],
        (10**10, lin.size * 6, lin.size),
        (meta, gz2, gzp2, gx3, gy, interp, lin, first, second, fine_modes, owned), after, onto,
    )


def interp_tables(plan):
    fine = host_interp(plan.nz).T
    lo, mid = plan.nz // 4, plan.nz // 2
    table = np.zeros((2, plan.pairs, 2 * LANES, 2 * plan.nz), np.float32)
    for c2 in range(2):
        for x in range(plan.planes):
            side = x % 2
            spot = table[c2, x // 2, :, side * plan.nz:(side + 1) * plan.nz]
            spot[side * mid:(side + 1) * mid] = fine[lo:lo + mid]
            at = LANES + c2 * 2 * plan.planes + 2 * x
            spot[at] = fine[lo - 1]
            spot[at + 1] = fine[lo + mid]
    return table.reshape(2 * plan.pairs, 2 * LANES, 2 * plan.nz).astype(ml_dtypes.bfloat16)


def pointwise(plan, lin_local, bias_local, ch_id, wide=16):
    size = plan.ch * wide
    eye = jnp.eye(wide, dtype=F32)
    kron = jnp.einsum("io,ab->oaib", lin_local.astype(F32), eye).astype(BF)
    kron = kron.reshape(size, 2, size).transpose(1, 0, 2)
    w_own = lax.dynamic_index_in_dim(kron, ch_id, 0, keepdims=False)
    w_far = lax.dynamic_index_in_dim(kron, 1 - ch_id, 0, keepdims=False)
    bias_rows = jnp.repeat(bias_local.astype(F32), wide)[:, None]
    return w_own, w_far, jnp.broadcast_to(bias_rows, (size, 2 * LANES))


def fast_body(plan, field, mode_local, lin_local, bias_local, own_row):
    slabs, planes, ch, modes = plan.slabs, plan.planes, plan.ch, plan.modes
    slab_id = lax.axis_index("slab")
    pool_id = lax.axis_index("pool")
    ch_id = lax.axis_index("ch")
    fwd_x, inv_x = host_tables(plan.nx, modes)
    fwd_y, inv_y = host_tables(plan.ny, modes)
    fwd_z, inv_z = host_tables(plan.nz, modes)
    esel = edge_select(plan).reshape(2 * plan.pairs, 2 * plan.nz, LANES)
    esel = esel.astype(ml_dtypes.bfloat16)

    above = shifted(own_row, "slab", 1)
    below = shifted(own_row, "slab", -1)
    far_field = swapped(field, "ch", 0)
    meta = jnp.concatenate([
        own_row,
        jnp.where(slab_id > 0, above, -1),
        jnp.where(slab_id < slabs - 1, below, -1),
        jnp.stack([slab_id, pool_id]).astype(jnp.int32),
    ])

    sent = gate(run_forward(plan, fwd_y, two_of(fwd_z.T), field), (meta,))
    pencils = lax.all_to_all(sent, "slab", split_axis=0, concat_axis=0, tiled=True)

    both = ("pool", "slab")
    firsts, packs, last = [], [], sent
    for group in plan.groups:
        last = run_pack(plan, meta, esel, field, group, False, (last,))[0]
        firsts.append(lax.ppermute(last, "pool", [(0, 1)]))
        last, to_right, to_left = run_pack(plan, meta, esel, field, group, True, (last,))
        packs.append((
            last,
            lax.ppermute(to_right, both, [(i, i + 1) for i in range(slabs - 1)]),
            lax.ppermute(to_left, both, [(i + 1, i) for i in range(slabs - 1)]),
        ))

    partial = run_mix(plan, fwd_x, mode_local, pencils, (last,))
    halves = partial.reshape(2, ch, modes, plan.q)
    mine = lax.dynamic_index_in_dim(halves, ch_id, 0, keepdims=False)
    theirs = lax.dynamic_index_in_dim(halves, 1 - ch_id, 0, keepdims=False)
    mixed = run_sum(plan, mine, swapped(theirs, "ch", 0), (firsts[0],))

    back = run_back_x(plan, inv_x, mixed)
    owned = lax.all_to_all(back, "slab", split_axis=0, concat_axis=0, tiled=True)

    w_own, w_far, bias_rows = pointwise(plan, lin_local, bias_local, ch_id)
    lin = run_linear(plan, w_own, w_far, bias_rows, field, far_field, (back,))

    lead = 2 * plan.groups[0][1]
    rest = ch - lead
    hop = lax.ppermute(mixed[:lead], "pool", [(1, 0)])
    here = jnp.where(pool_id == 0, hop, mixed[ch - lead:])
    here = gate(here, (back,) + packs[0][1:])
    here = lax.all_gather(here, "slab", axis=0, tiled=False)
    seconds, last = [], lin
    for second, from_left, from_right in packs:
        last = run_assemble(plan, meta, second, from_left, from_right, (last, firsts[-1]))
        seconds.append(lax.ppermute(last, "pool", [(0, 1)]))
    over = gate(here[:, lead - rest:], (last,))
    gathered = [here, lax.ppermute(over, "pool", [(1, 0)])]

    to_coarse = 0.5 * host_interp(plan.nz)
    gzp = (inv_z.T.astype(np.float32) @ to_coarse).astype(ml_dtypes.bfloat16)
    padded = np.pad(inv_x.reshape(slabs, planes, modes), ((1, 1), (0, 0), (0, 0)))
    gx3 = lax.dynamic_slice_in_dim(jnp.asarray(padded), slab_id, 3, 0)
    gx3 = gx3.reshape(3 * planes, modes)
    out = None
    for group, first_in, second, modes_in in zip(plan.groups, firsts, seconds, gathered):
        out = run_final(plan, meta, two_of(inv_z.T), two_of(gzp), gx3, inv_y, interp_tables(plan),
                        lin, first_in, second, modes_in, owned, group, out)
    return out


def plain_body(field, mode_local, lin_local, bias_local, own_row):
    bias_local = bias_local.astype(jnp.float32)
    own_ch, planes, y_cells, z_cells = field.shape
    modes = mode_local.shape[2]
    x_cells = planes * lax.axis_size("slab")
    block_count = own_row.shape[0]
    block_rows = y_cells // block_count
    slab_id = lax.axis_index("slab")
    is_coarse = lax.axis_index("pool") == 0
    fwd_x, inv_x = tables(x_cells, modes)
    fwd_y, inv_y = tables(y_cells, modes)
    fwd_z, inv_z = tables(z_cells, modes)
    pmat = interp_table(z_cells)
    z_table = jnp.where(is_coarse, pmat.T.astype(jnp.bfloat16), (0.5 * pmat).astype(jnp.bfloat16))
    block_ids = jnp.arange(block_count, dtype=jnp.int32)
    here_mask = (own_row == slab_id).astype(jnp.float32)[None, None, :, None]
    side_rows = [shifted(own_row, "slab", shift_by) for shift_by in (1, -1)]
    all_channels = lax.all_gather(field, "ch", axis=0, tiled=True)
    along_y = jnp.einsum("cxyz,my->cxmz", field, fwd_y, preferred_element_type=jnp.float32).astype(
        jnp.bfloat16
    )
    along_z = jnp.einsum(
        "cxmz,kz->cxmk", along_y, fwd_z, preferred_element_type=jnp.float32
    ).astype(jnp.bfloat16)
    along_z = along_z.reshape(own_ch, planes, modes * modes)
    pencils = lax.all_to_all(along_z, "slab", split_axis=2, concat_axis=1, tiled=True)
    coeffs = jnp.einsum("cxq,nx->cnq", pencils, fwd_x, preferred_element_type=jnp.float32).astype(
        jnp.bfloat16
    )
    partial_mix = jnp.einsum(
        "inq,ionq->onq", coeffs, mode_local, preferred_element_type=jnp.float32
    )
    mixed = lax.psum_scatter(
        partial_mix.astype(jnp.bfloat16), "ch", scatter_dimension=0, tiled=True
    )
    back_x = jnp.einsum("onq,xn->oxq", mixed, inv_x, preferred_element_type=jnp.float32).astype(
        jnp.bfloat16
    )
    back_x = lax.all_to_all(back_x, "slab", split_axis=1, concat_axis=2, tiled=True).reshape(
        own_ch, planes, modes, modes
    )
    back_z = jnp.einsum("cxmk,zk->cxmz", back_x, inv_z, preferred_element_type=jnp.float32).astype(
        jnp.bfloat16
    )
    spec = jnp.einsum("cxmz,ym->cxyz", back_z, inv_y, preferred_element_type=jnp.float32)
    flat_all = all_channels.reshape(all_channels.shape[0], planes * y_cells * z_cells)
    linear = jnp.einsum("io,ir->or", lin_local, flat_all, preferred_element_type=jnp.float32)
    linear = linear.reshape(own_ch, planes, y_cells, z_cells)
    anchor = jnp.where(is_coarse, field, spec.astype(jnp.bfloat16))
    payload = jnp.dot(anchor, z_table, preferred_element_type=jnp.float32).astype(jnp.bfloat16)
    partner = swapped(payload, "pool", 0)
    partner_blocks = partner.reshape(own_ch, planes, block_count, block_rows * z_cells)
    coupling = partner_blocks.astype(jnp.float32) * here_mask
    for shift_by, dest_row in ((1, side_rows[1]), (-1, side_rows[0])):
        sending = jnp.where(is_coarse, own_row == slab_id + shift_by, dest_row == slab_id).astype(
            jnp.int32
        )
        position = jnp.cumsum(sending) - 1
        slots = jnp.arange(HOP, dtype=jnp.int32)[:, None]
        select = (sending[None, :] == 1) & (position[None, :] == slots)
        packed = jnp.einsum(
            "hb,cxbr->cxhr",
            select.astype(jnp.bfloat16),
            partner_blocks,
            preferred_element_type=jnp.float32,
        ).astype(jnp.bfloat16)
        packed_ids = jnp.where(
            jnp.any(select, axis=1),
            jnp.sum(select.astype(jnp.int32) * block_ids[None, :], axis=1),
            -1,
        )
        arrived, arrived_ids = shifted((packed, packed_ids), "slab", shift_by)
        placing = (arrived_ids[:, None] == block_ids[None, :]).astype(jnp.bfloat16)
        coupling = coupling + jnp.einsum(
            "hb,cxhr->cxbr", placing, arrived, preferred_element_type=jnp.float32
        )
    total = (
        spec
        + linear
        + bias_local[:, None, None, None]
        + coupling.reshape(own_ch, planes, y_cells, z_cells)
    )
    return jax.nn.gelu(total, approximate=False).astype(jnp.bfloat16)


def body(fields, mode_weights, lin_weights, bias, source):
    args = (fields[0], mode_weights[0], lin_weights[0], bias[0], source[0])
    plan = Plan(args[0], args[1], args[4], lax.axis_size("slab"))
    if plan.fits():
        return fast_body(plan, *args)[None]
    return plain_body(*args)[None]


def solution(mesh):
    return jax.shard_map(
        body,
        mesh=mesh,
        in_specs=(
            P("pool", "ch", "slab", None, None),
            P("pool", "ch", None, None, "slab"),
            P("pool", None, "ch"),
            P("pool", "ch"),
            P("slab", None),
        ),
        out_specs=P("pool", "ch", "slab", None, None),
        check_vma=False,
    )
```

```python
import functools

import jax
import jax.numpy as jnp
import ml_dtypes
import numpy as np
from jax import lax
from jax.experimental import pallas as pl
from jax.experimental.pallas import tpu as pltpu
from jax.sharding import PartitionSpec as P

HOP = 2
LANES = 128
BF = jnp.bfloat16
F32 = jnp.float32
ERF_POLY = (
    7.97884216e-01, 3.63342835e-02, -3.31299940e-05, -5.52401584e-05,
    3.96910946e-06, -1.33446410e-07, 1.80561642e-09,
)


def shifted(value, axis, steps):
    count = lax.axis_size(axis)
    leading, last = (max(0, -steps), min(count, count - steps))
    return lax.ppermute(value, axis, [(source, source + steps) for source in range(leading, last)])


def swapped(value, axis, apart):
    mask = 2**apart
    pairs = [(source, source ^ mask) for source in range(lax.axis_size(axis))]
    return lax.ppermute(value, axis, pairs)


def tables(length, modes):
    cells = jnp.arange(length, dtype=jnp.float32)
    order = jnp.arange(modes, dtype=jnp.int32)
    half = modes // 2
    freq = jnp.where(order < half, order, order - half + 1).astype(jnp.float32)
    angle = 2.0 * jnp.pi * freq[:, None] * cells[None, :] / length
    forward = jnp.where((order < half)[:, None], jnp.cos(angle), jnp.sin(angle))
    return (forward.astype(jnp.bfloat16), (forward.T * (2.0 / length)).astype(jnp.bfloat16))


def interp_table(length):
    fine_idx = jnp.arange(length, dtype=jnp.int32)[:, None]
    coarse_idx = jnp.arange(length, dtype=jnp.int32)[None, :]
    centre = length // 4 + fine_idx // 2
    second = centre - 1 + 2 * (fine_idx % 2)
    return 0.75 * (coarse_idx == centre).astype(jnp.float32) + 0.25 * (coarse_idx == second).astype(
        jnp.float32
    )


def host_interp(length):
    fine = np.arange(length)[:, None]
    coarse = np.arange(length)[None, :]
    centre = length // 4 + fine // 2
    second = centre - 1 + 2 * (fine % 2)
    return (0.75 * (coarse == centre) + 0.25 * (coarse == second)).astype(np.float32)


def host_tables(length, modes):
    cells = np.arange(length, dtype=np.float32)
    order = np.arange(modes)
    half = modes // 2
    freq = np.where(order < half, order, order - half + 1).astype(np.float32)
    angle = np.float32(2.0 * np.pi) * freq[:, None] * cells[None, :] / np.float32(length)
    forward = np.where((order < half)[:, None], np.cos(angle), np.sin(angle)).astype(np.float32)
    inverse = forward.T * np.float32(2.0 / length)
    return forward.astype(ml_dtypes.bfloat16), inverse.astype(ml_dtypes.bfloat16)


def two_of(table):
    zero = np.zeros_like(table)
    return np.block([[table, zero], [zero, table]])


def dot(left, right):
    return jnp.dot(left, right, preferred_element_type=F32)


def gelu(v):
    square = jnp.minimum(v * v, 36.0)
    poly = ERF_POLY[-1]
    for coef in ERF_POLY[-2::-1]:
        poly = poly * square + coef
    half = 0.5 * v
    return half + half * jnp.tanh(v * poly)


class Plan:
    def __init__(self, field, mode_local, own_row, slabs):
        self.ch, self.planes, self.ny, self.nz = field.shape
        self.modes, self.q = mode_local.shape[2], mode_local.shape[3]
        self.outs = mode_local.shape[1]
        self.blocks = own_row.shape[0]
        self.slabs = slabs
        self.nx = self.planes * slabs
        self.rows = self.ny // self.blocks
        self.half = (self.blocks - 2 * HOP) * self.rows
        self.hop = HOP * self.rows
        self.group = self.modes // slabs if self.modes % slabs == 0 else 0
        self.pairs = self.planes // 2
        self.mid_rows = 2 * self.pairs * self.half
        self.pack_rows = self.mid_rows + self.half
        self.edge_rows = -(-self.hop // 16) * 16
        self.nb_rows = self.pairs * 2 * self.hop + self.edge_rows
        total = self.ch // 2
        counts = [-(-total // 2), total // 2]
        self.groups = [(sum(counts[:i]), count) for i, count in enumerate(counts) if count]
        self.step = self.planes + 8 if self.planes % 16 == 0 else self.planes
        self.depth = 4 * self.modes + 8

    def chan_spec(self):
        return pl.BlockSpec((1, self.planes, self.ny, self.nz), lambda c: (c, 0, 0, 0))

    def fits(self):
        return (
            self.group >= 2
            and self.group % 2 == 0
            and self.slabs & (self.slabs - 1) == 0
            and self.nz == LANES
            and 2 * self.modes == LANES
            and self.ch % 2 == 0
            and self.outs == 2 * self.ch
            and self.planes % 16 == 0
            and 4 * self.planes <= LANES
            and self.ny % 16 == 0
            and self.blocks == 4 * HOP
            and self.half % 16 == 0
            and self.half == 2 * self.hop
            and self.hop % 8 == 0
            and self.hop <= 64
            and self.q == self.group * self.modes
        )


def listing(meta, plan):
    nb = plan.blocks
    slab = meta[3 * nb]
    one, zero = jnp.int32(1), jnp.int32(0)
    row = [meta[b] for b in range(nb)]
    left = [jnp.where((row[b] == slab - 1) & (row[b] >= 0), one, zero) for b in range(nb)]
    right = [jnp.where(row[b] == slab + 1, one, zero) for b in range(nb)]
    listed = [jnp.where(row[b] >= 0, one, zero) for b in range(nb)]
    near = [1 - left[b] - right[b] for b in range(nb)]
    total = functools.reduce(lambda a, b: a + b, near)
    place, rank_l, rank_r = [], [], []
    n_near, n_far, n_l, n_r = zero, total, zero, zero
    for b in range(nb):
        place.append(jnp.where(near[b] == 1, n_near, n_far))
        rank_l.append(n_l)
        rank_r.append(n_r)
        n_near, n_far = n_near + near[b], n_far + 1 - near[b]
        n_l, n_r = n_l + left[b], n_r + right[b]
    return dict(slab=slab, left=left, right=right, listed=listed, near=near, place=place,
                rank_l=rank_l, rank_r=rank_r)


def sends(meta, plan, which):
    nb = plan.blocks
    slab = meta[3 * nb]
    ask = [jnp.where(meta[which * nb + b] == slab, jnp.int32(1), jnp.int32(0)) for b in range(nb)]
    rank, count = [], jnp.int32(0)
    for b in range(nb):
        rank.append(jnp.where(ask[b] == 1, count, jnp.int32(-1)))
        count = count + ask[b]
    return rank


def steps_of(index, size, count):
    out = jnp.zeros_like(index)
    for k in range(1, count):
        out = out + jnp.where(index >= k * size, jnp.int32(1), jnp.int32(0))
    return out


def by_block(block, values):
    out = jnp.full_like(block, -1)
    for b, value in enumerate(values):
        out = jnp.where(block == b, value, out)
    return out


def chosen(mask):
    return jnp.where(mask, 1.0, 0.0).astype(F32)


def row_col(rows, cols):
    shape = (rows, cols)
    return lax.broadcasted_iota(jnp.int32, shape, 0), lax.broadcasted_iota(jnp.int32, shape, 1)


def forward_kernel(plan, fy, fz2, u, out, scr):
    planes, modes, step = plan.planes, plan.modes, plan.step
    for xp in range(plan.pairs):
        both = jnp.concatenate([u[0, 2 * xp], u[0, 2 * xp + 1]], axis=1)
        along = dot(fy[...], both)
        for side in range(2):
            scr[pl.ds(2 * xp + side, modes, stride=step), :] = along[
                :, side * LANES:(side + 1) * LANES
            ]
    for d in range(plan.slabs):
        lefts = []
        for jp in range(plan.group // 2):
            start = (d * plan.group + 2 * jp) * step
            lefts.append(jnp.concatenate(
                [scr[start:start + planes], scr[start + step:start + step + planes]], axis=1
            ))
        done = dot(jnp.concatenate(lefts, axis=0).astype(BF), fz2[...]).astype(BF)
        for jp in range(plan.group // 2):
            out[d, 0, :, jp * LANES:(jp + 1) * LANES] = done[jp * planes:(jp + 1) * planes]


def pack(plan, sel, esel, u, store, store_edges):
    lo, mid = plan.nz // 4, plan.nz // 2
    edges = jnp.zeros((plan.ny, LANES), F32)
    for c2 in range(2):
        for double in range(plan.pairs // 2):
            mids = []
            for i in range(2):
                x = 4 * double + 2 * i
                mids += [u[c2, x, :, lo:lo + mid], u[c2, x + 1, :, lo:lo + mid]]
            packed = dot(sel[...], jnp.concatenate(mids, axis=1))
            store(c2, double, [packed[:, :LANES], packed[:, LANES:]])
        for xp in range(plan.pairs):
            both = jnp.concatenate([u[c2, 2 * xp], u[c2, 2 * xp + 1]], axis=1)
            edges = edges + dot(both, esel[c2 * plan.pairs + xp])
    store_edges(dot(sel[...], edges.astype(BF)).astype(BF))


def picks(plan, info, first):
    nb = plan.blocks
    row, col = row_col(plan.half, plan.ny)
    block = steps_of(col, plan.rows, nb)
    slot = steps_of(row, plan.rows, 2 * HOP) + first
    same = row - (slot - first) * plan.rows == col - block * plan.rows
    near = by_block(block, info["near"]) == 1
    return chosen(same & near & (by_block(block, info["place"]) == slot)).astype(BF)


def pack_first_kernel(plan, meta, esel, u, h1, sel):
    half = plan.half

    @pl.when(pl.program_id(0) == 0)
    def _():
        sel[...] = picks(plan, listing(meta, plan), 0)

    def store(c2, double, tiles):
        for i, tile in enumerate(tiles):
            at = (c2 * plan.pairs + 2 * double + i) * half
            h1[0, at:at + half, :] = tile.astype(BF)

    def store_edges(packed):
        h1[0, plan.mid_rows:] = packed

    pack(plan, sel, esel, u, store, store_edges)


def pack_rest_kernel(plan, meta, esel, u, h2, right, left, sel):
    half, hop, nb = plan.half, plan.hop, plan.blocks
    pad = plan.edge_rows

    @pl.when(pl.program_id(0) == 0)
    def _():
        sel[0:half] = picks(plan, listing(meta, plan), nb - 2 * HOP)
        row, col = row_col(pad, plan.ny)
        block = steps_of(col, plan.rows, nb)
        slot = steps_of(row, plan.rows, HOP + 1)
        same = (row - slot * plan.rows == col - block * plan.rows) & (slot < HOP)
        for which in range(2):
            rank = by_block(block, sends(meta, plan, 2 - which))
            start = half + which * pad
            sel[start:start + pad] = chosen(same & (rank == slot)).astype(BF)

    def store(c2, double, tiles):
        for i, tile in enumerate(tiles):
            at = (c2 * plan.pairs + 2 * double + i) * half
            h2[0, at:at + half, :] = tile[0:half].astype(BF)
        at = (c2 * plan.pairs // 2 + double) * 2 * hop
        for ref, start in ((right, half), (left, half + pad)):
            ref[0, at:at + 2 * hop, :] = jnp.concatenate(
                [tile[start:start + hop] for tile in tiles], axis=0
            ).astype(BF)

    def store_edges(packed):
        h2[0, plan.mid_rows:] = packed[0:half]
        right[0, 2 * plan.pairs * hop:] = packed[half:half + pad]
        left[0, 2 * plan.pairs * hop:] = packed[half + pad:half + 2 * pad]

    pack(plan, sel, esel, u, store, store_edges)


def assemble_kernel(plan, meta, h2, from_left, from_right, out, sel, edge_sel):
    half, hop, nb = plan.half, plan.hop, plan.blocks
    pad = plan.edge_rows

    @pl.when(pl.program_id(0) == 0)
    def _():
        info = listing(meta, plan)

        def build(width, period, offset):
            row, col = row_col(half, 2 * width)
            side = steps_of(col, width, 2)
            within = col - side * width
            part = steps_of(within, period, max(1, width // period))
            inner = within - part * period
            slot = steps_of(inner, plan.rows, HOP + 1)
            target = steps_of(row, plan.rows, 2 * HOP)
            same = (row - target * plan.rows == inner - slot * plan.rows) & (part == offset)
            mask = jnp.zeros((half, 2 * width), F32)
            for b in range(nb):
                place = info["place"][b] - (nb - 2 * HOP)
                hit = same & (target == place)
                mask = mask + chosen(
                    hit & (side == 0) & (slot == info["rank_l"][b]) & (info["left"][b] == 1)
                ) + chosen(
                    hit & (side == 1) & (slot == info["rank_r"][b]) & (info["right"][b] == 1)
                )
            return mask.astype(BF)

        for offset in range(2):
            sel[offset] = build(2 * hop, hop, offset)
        edge_sel[...] = build(pad, pad, 0)

    @pl.loop(0, plan.pairs, unroll=4)
    def _(double):
        at = pl.multiple_of(double * 2 * hop, 16)
        sides = jnp.concatenate(
            [from_left[0, pl.ds(at, 2 * hop), :], from_right[0, pl.ds(at, 2 * hop), :]], axis=0
        )
        for i in range(2):
            to = pl.multiple_of((2 * double + i) * half, 16)
            own = h2[0, pl.ds(to, half), :].astype(F32)
            out[0, pl.ds(to, half), :] = (own + dot(sel[i], sides)).astype(BF)

    sides = jnp.concatenate(
        [from_left[0, 2 * plan.pairs * hop:], from_right[0, 2 * plan.pairs * hop:]], axis=0
    )
    own = h2[0, plan.mid_rows:].astype(F32)
    out[0, plan.mid_rows:] = (own + dot(edge_sel[...], sides)).astype(BF)


def linear_kernel(plan, w_own, w_far, bias, own, far, out):
    ch = plan.ch
    wide = w_own.shape[0] // ch
    for xp in range(own.shape[1] // 2):
        for g in range(plan.ny // wide):
            def tile(ref):
                sides = [
                    ref[:, 2 * xp + i, g * wide:(g + 1) * wide, :].reshape(ch * wide, LANES)
                    for i in range(2)
                ]
                return jnp.concatenate(sides, axis=1)

            total = dot(w_own[...], tile(own)) + dot(w_far[...], tile(far)) + bias[...]
            total = total.astype(BF)
            for i in range(2):
                out[:, 2 * xp + i, g * wide:(g + 1) * wide, :] = total[
                    :, i * LANES:(i + 1) * LANES
                ].reshape(ch, wide, LANES)


def mix_kernel(plan, fx, weights, pencils, out, coeffs):
    step = pl.program_id(0)
    ch, rows = plan.ch, weights.shape[2]

    @pl.when(step == 0)
    def _():
        @pl.loop(0, ch)
        def _(c):
            column = jnp.concatenate([pencils[d, c] for d in range(plan.slabs)], axis=0)
            coeffs[c] = dot(fx[...], column).astype(BF).astype(F32)

    start = pl.multiple_of(step * rows, rows)

    @pl.loop(0, plan.outs)
    def _(o):
        total = weights[0, o].astype(F32) * coeffs[0, pl.ds(start, rows), :]
        for c in range(1, ch):
            total = total + weights[c, o].astype(F32) * coeffs[c, pl.ds(start, rows), :]
        out[o] = total.astype(BF)


def sum_kernel(plan, mine, got, out):
    out[...] = (mine[...].astype(F32) + got[...].astype(F32)).astype(BF)


def back_x_kernel(plan, gx, mixed, out):
    done = dot(gx[...], mixed[0]).astype(BF)
    for k in range(plan.slabs):
        out[k, 0] = done[k * plan.planes:(k + 1) * plan.planes]


def final_kernel(plan, meta, gz2, gzp2, gx3, gy, interp, lin, h1, h2, modes0, owns, out, scr, wide,
                 place):
    nb, slabs, planes, modes, half = plan.blocks, plan.slabs, plan.planes, plan.modes, plan.half
    depth = plan.depth
    coarse = meta[3 * nb + 1] == 0
    step = pl.program_id(0)

    @pl.when(step == 0)
    def _():
        info = listing(meta, plan)
        row, col = row_col(plan.ny, modes)
        block = steps_of(row, plan.rows, nb)
        wide[:, 0:modes] = gy[...]
        for which, base in ((1, 1), (2, 0), (3, 2)):
            fed = by_block(block, [meta[base * nb + b] for b in range(nb)]) == info["slab"]
            wide[:, which * modes:(which + 1) * modes] = jnp.where(
                fed, gy[...].astype(F32), 0.0
            ).astype(BF)
        row, col = row_col(plan.ny, plan.ny)
        block = steps_of(row, plan.rows, nb)
        slot = steps_of(col, plan.rows, nb)
        same = row - block * plan.rows == col - slot * plan.rows
        listed = by_block(block, info["listed"]) == 1
        place[...] = chosen(same & listed & (by_block(block, info["place"]) == slot)).astype(BF)

    for d in range(slabs):
        left = jnp.concatenate(
            [owns[d, 0, :, jp * LANES:(jp + 1) * LANES] for jp in range(plan.group // 2)], axis=0
        )
        done = dot(left, gz2[...])
        for jp in range(plan.group // 2):
            for i in range(2):
                m = d * plan.group + 2 * jp + i
                scr[pl.ds(m, planes, stride=depth), :] = done[
                    jp * planes:(jp + 1) * planes, i * LANES:(i + 1) * LANES
                ]

    @pl.when(coarse)
    def _():
        for d in range(slabs):
            beside = dot(gx3[...], modes0[d, 0]).astype(BF)
            left = jnp.concatenate(
                [beside[:, jp * LANES:(jp + 1) * LANES] for jp in range(plan.group // 2)], axis=0
            )
            done = dot(left, gzp2[...])
            for jp in range(plan.group // 2):
                for which in range(3):
                    at = (jp * 3 + which) * planes
                    for i in range(2):
                        m = (which + 1) * modes + d * plan.group + 2 * jp + i
                        scr[pl.ds(m, planes, stride=depth), :] = done[
                            at:at + planes, i * LANES:(i + 1) * LANES
                        ]

    def emit(xp, total):
        for i in range(2):
            for r in range(0, plan.ny, 16):
                v = total[r:r + 16, i * LANES:(i + 1) * LANES] + lin[
                    0, 2 * xp + i, r:r + 16, :
                ].astype(F32)
                out[0, 2 * xp + i, r:r + 16, :] = gelu(v).astype(BF)

    def spread(xp, count):
        sides = []
        for i in range(2):
            at = pl.multiple_of((2 * xp + i) * depth, 8)
            sides.append(scr[pl.ds(at, count), :])
        return jnp.concatenate(sides, axis=1).astype(BF)

    @pl.when(coarse)
    def _():
        @pl.loop(0, plan.pairs, unroll=8)
        def _(xp):
            emit(xp, dot(wide[...], spread(xp, 4 * modes)))

    @pl.when(jnp.logical_not(coarse))
    def _():
        c2 = lax.rem(step, 2)

        @pl.loop(0, plan.pairs, unroll=8)
        def _(xp):
            at = pl.multiple_of((c2 * plan.pairs + xp) * half, 16)
            table = interp[c2 * plan.pairs + xp]
            parts = []
            for ref in (h1, h2):
                packed = jnp.concatenate(
                    [ref[0, pl.ds(at, half), :], ref[0, plan.mid_rows:]], axis=1
                )
                parts.append(dot(packed, table).astype(BF))
            fed = dot(place[...], jnp.concatenate(parts, axis=0))
            emit(xp, fed + dot(gy[...], spread(xp, modes)))


def whole(shape):
    return pl.BlockSpec(shape, lambda *_: (0,) * len(shape))


SCALARS = pl.BlockSpec(memory_space=pltpu.SMEM)


def edge_select(plan):
    lo, mid = plan.nz // 4, plan.nz // 2
    sel = np.zeros((2, plan.planes, plan.nz, LANES), np.float32)
    for c2 in range(2):
        for x in range(plan.planes):
            at = c2 * 2 * plan.planes + 2 * x
            sel[c2, x, lo - 1, at] = 1.0
            sel[c2, x, lo + mid, at + 1] = 1.0
    return sel


def call(kernel, plan, grid, in_specs, out_specs, out_shape, scratch, cost, args, after=(),
         onto=None):
    count = len(args)
    aliases = {}
    if onto is not None:
        aliases = {count: 0}
        after = (onto,) + tuple(after)

    def run(*refs):
        kernel(plan, *refs[:count], *refs[count + len(after):])

    flops, traffic, special = cost
    return pl.pallas_call(
        run,
        grid=grid,
        in_specs=in_specs + [pl.BlockSpec(memory_space=pl.ANY)] * len(after),
        out_specs=out_specs,
        out_shape=out_shape,
        scratch_shapes=scratch,
        input_output_aliases=aliases,
        compiler_params=pltpu.CompilerParams(vmem_limit_bytes=56 * 2**20),
        cost_estimate=pl.CostEstimate(
            flops=1000, bytes_accessed=1000, transcendentals=0
        ),
    )(*args, *after)


def gate(value, after):
    anywhere = pl.BlockSpec(memory_space=pl.ANY)
    return pl.pallas_call(
        lambda *refs: None,
        in_specs=[anywhere] * (1 + len(after)),
        out_specs=anywhere,
        out_shape=jax.ShapeDtypeStruct(value.shape, value.dtype),
        input_output_aliases={0: 0},
    )(value, *after)


def run_forward(plan, fy, fz2, field, after=()):
    shape = (plan.slabs, plan.ch, plan.planes, plan.q)
    return call(
        forward_kernel, plan, (plan.ch,),
        [whole(fy.shape), whole(fz2.shape), plan.chan_spec()],
        pl.BlockSpec((plan.slabs, 1, plan.planes, plan.q), lambda c: (0, c, 0, 0)),
        jax.ShapeDtypeStruct(shape, BF),
        [pltpu.VMEM((plan.modes * plan.step, LANES), F32)],
        (10**9, field.size * 2, 0), (fy, fz2, field), after,
    )


def run_pack(plan, meta, esel, field, group, near, after=()):
    start, count = group
    full = jax.ShapeDtypeStruct((count, plan.pack_rows, LANES), BF)
    part = jax.ShapeDtypeStruct((count, plan.nb_rows, LANES), BF)
    shapes = [full, part, part] if near else [full]
    rows = plan.half + 2 * plan.edge_rows if near else plan.half
    return call(
        pack_rest_kernel if near else pack_first_kernel, plan, (count,),
        [SCALARS, whole(esel.shape),
         pl.BlockSpec((2,) + field.shape[1:], lambda c: (c + start, 0, 0, 0))],
        [pl.BlockSpec((1,) + shape.shape[1:], lambda c: (c, 0, 0)) for shape in shapes], shapes,
        [pltpu.VMEM((rows, plan.ny), BF)],
        (10**9, field.size * 3, 0), (meta, esel, field), after,
    )


def run_assemble(plan, meta, second, from_left, from_right, after=()):
    pack_spec = pl.BlockSpec((1, plan.pack_rows, LANES), lambda c: (c, 0, 0))
    near_spec = pl.BlockSpec((1, plan.nb_rows, LANES), lambda c: (c, 0, 0))
    return call(
        assemble_kernel, plan, (second.shape[0],),
        [SCALARS, pack_spec, near_spec, near_spec], pack_spec,
        jax.ShapeDtypeStruct(second.shape, BF),
        [pltpu.VMEM((2, plan.half, 4 * plan.hop), BF),
         pltpu.VMEM((plan.half, 2 * plan.edge_rows), BF)],
        (10**9, second.size * 6, 0), (meta, second, from_left, from_right), after,
    )


def run_linear(plan, w_own, w_far, bias_rows, field, far_field, after=()):
    per = 4
    spec = pl.BlockSpec((plan.ch, per) + field.shape[2:], lambda x: (0, x, 0, 0))
    return call(
        linear_kernel, plan, (plan.planes // per,),
        [whole(w_own.shape), whole(w_far.shape), whole(bias_rows.shape), spec, spec],
        spec, jax.ShapeDtypeStruct(field.shape, BF), [],
        (2 * 10**10, field.size * 6, 0), (w_own, w_far, bias_rows, field, far_field), after,
    )


def run_mix(plan, fx, weights, pencils, after=()):
    rows = 16
    return call(
        mix_kernel, plan, (plan.modes // rows,),
        [whole(fx.shape),
         pl.BlockSpec((plan.ch, plan.outs, rows, plan.q), lambda n: (0, 0, n, 0)),
         whole(pencils.shape)],
        pl.BlockSpec((plan.outs, rows, plan.q), lambda n: (0, n, 0)),
        jax.ShapeDtypeStruct((plan.outs, plan.modes, plan.q), BF),
        [pltpu.VMEM((plan.ch, plan.modes, plan.q), F32)],
        (10**9, weights.size * 2, 0), (fx, weights, pencils), after,
    )


def run_sum(plan, mine, got, after=()):
    return call(
        sum_kernel, plan, (1,), [whole(mine.shape), whole(mine.shape)], whole(mine.shape),
        jax.ShapeDtypeStruct(mine.shape, BF), [], (1, 1, 0), (mine, got), after,
    )


def run_back_x(plan, gx, mixed, after=()):
    return call(
        back_x_kernel, plan, (plan.ch,),
        [whole(gx.shape), pl.BlockSpec((1, plan.modes, plan.q), lambda c: (c, 0, 0))],
        pl.BlockSpec((plan.slabs, 1, plan.planes, plan.q), lambda c: (0, c, 0, 0)),
        jax.ShapeDtypeStruct((plan.slabs, plan.ch, plan.planes, plan.q), BF), [],
        (10**9, mixed.size * 10, 0), (gx, mixed), after,
    )


def run_final(plan, meta, gz2, gzp2, gx3, gy, interp, lin, first, second, fine_modes, owned, group,
              onto=None, after=()):
    start, count = group
    at = 2 * start
    chan_spec = pl.BlockSpec((1,) + lin.shape[1:], lambda c: (c + at, 0, 0, 0))
    pair_spec = pl.BlockSpec((1, plan.pack_rows, LANES), lambda c: (c // 2, 0, 0))
    return call(
        final_kernel, plan, (2 * count,),
        [SCALARS, whole(gz2.shape), whole(gzp2.shape), whole(gx3.shape), whole(gy.shape),
         whole(interp.shape), chan_spec, pair_spec, pair_spec,
         pl.BlockSpec((plan.slabs, 1, plan.modes, plan.q), lambda c: (0, c, 0, 0)),
         pl.BlockSpec((plan.slabs, 1, plan.planes, plan.q), lambda c: (0, c + at, 0, 0))],
        chan_spec, jax.ShapeDtypeStruct(lin.shape, BF),
        [pltpu.VMEM((plan.planes * plan.depth, LANES), F32),
         pltpu.VMEM((plan.ny, 4 * plan.modes), BF),
         pltpu.VMEM((plan.ny, plan.ny), BF)],
        (10**10, lin.size * 6, lin.size),
        (meta, gz2, gzp2, gx3, gy, interp, lin, first, second, fine_modes, owned), after, onto,
    )


def interp_tables(plan):
    fine = host_interp(plan.nz).T
    lo, mid = plan.nz // 4, plan.nz // 2
    table = np.zeros((2, plan.pairs, 2 * LANES, 2 * plan.nz), np.float32)
    for c2 in range(2):
        for x in range(plan.planes):
            side = x % 2
            spot = table[c2, x // 2, :, side * plan.nz:(side + 1) * plan.nz]
            spot[side * mid:(side + 1) * mid] = fine[lo:lo + mid]
            at = LANES + c2 * 2 * plan.planes + 2 * x
            spot[at] = fine[lo - 1]
            spot[at + 1] = fine[lo + mid]
    return table.reshape(2 * plan.pairs, 2 * LANES, 2 * plan.nz).astype(ml_dtypes.bfloat16)


def pointwise(plan, lin_local, bias_local, ch_id, wide=16):
    size = plan.ch * wide
    eye = jnp.eye(wide, dtype=F32)
    kron = jnp.einsum("io,ab->oaib", lin_local.astype(F32), eye).astype(BF)
    kron = kron.reshape(size, 2, size).transpose(1, 0, 2)
    w_own = lax.dynamic_index_in_dim(kron, ch_id, 0, keepdims=False)
    w_far = lax.dynamic_index_in_dim(kron, 1 - ch_id, 0, keepdims=False)
    bias_rows = jnp.repeat(bias_local.astype(F32), wide)[:, None]
    return w_own, w_far, jnp.broadcast_to(bias_rows, (size, 2 * LANES))


def fast_body(plan, field, mode_local, lin_local, bias_local, own_row):
    slabs, planes, ch, modes = plan.slabs, plan.planes, plan.ch, plan.modes
    slab_id = lax.axis_index("slab")
    pool_id = lax.axis_index("pool")
    ch_id = lax.axis_index("ch")
    fwd_x, inv_x = host_tables(plan.nx, modes)
    fwd_y, inv_y = host_tables(plan.ny, modes)
    fwd_z, inv_z = host_tables(plan.nz, modes)
    esel = edge_select(plan).reshape(2 * plan.pairs, 2 * plan.nz, LANES)
    esel = esel.astype(ml_dtypes.bfloat16)

    above = shifted(own_row, "slab", 1)
    below = shifted(own_row, "slab", -1)
    far_field = swapped(field, "ch", 0)
    meta = jnp.concatenate([
        own_row,
        jnp.where(slab_id > 0, above, -1),
        jnp.where(slab_id < slabs - 1, below, -1),
        jnp.stack([slab_id, pool_id]).astype(jnp.int32),
    ])

    sent = gate(run_forward(plan, fwd_y, two_of(fwd_z.T), field), (meta,))
    pencils = lax.all_to_all(sent, "slab", split_axis=0, concat_axis=0, tiled=True)

    both = ("pool", "slab")
    firsts, packs, last = [], [], sent
    for group in plan.groups:
        last = run_pack(plan, meta, esel, field, group, False, (last,))[0]
        firsts.append(lax.ppermute(last, "pool", [(0, 1)]))
        last, to_right, to_left = run_pack(plan, meta, esel, field, group, True, (last,))
        packs.append((
            last,
            lax.ppermute(to_right, both, [(i, i + 1) for i in range(slabs - 1)]),
            lax.ppermute(to_left, both, [(i + 1, i) for i in range(slabs - 1)]),
        ))

    partial = run_mix(plan, fwd_x, mode_local, pencils, (last,))
    halves = partial.reshape(2, ch, modes, plan.q)
    mine = lax.dynamic_index_in_dim(halves, ch_id, 0, keepdims=False)
    theirs = lax.dynamic_index_in_dim(halves, 1 - ch_id, 0, keepdims=False)
    mixed = run_sum(plan, mine, swapped(theirs, "ch", 0), (firsts[0],))

    back = run_back_x(plan, inv_x, mixed)
    owned = lax.all_to_all(back, "slab", split_axis=0, concat_axis=0, tiled=True)

    w_own, w_far, bias_rows = pointwise(plan, lin_local, bias_local, ch_id)
    lin = run_linear(plan, w_own, w_far, bias_rows, field, far_field, (back,))

    lead = 2 * plan.groups[0][1]
    rest = ch - lead
    hop = lax.ppermute(mixed[:lead], "pool", [(1, 0)])
    here = jnp.where(pool_id == 0, hop, mixed[ch - lead:])
    here = gate(here, (back,) + packs[0][1:])
    here = lax.all_gather(here, "slab", axis=0, tiled=False)
    seconds, last = [], lin
    for second, from_left, from_right in packs:
        last = run_assemble(plan, meta, second, from_left, from_right, (last, firsts[-1]))
        seconds.append(lax.ppermute(last, "pool", [(0, 1)]))
    over = gate(here[:, lead - rest:], (last,))
    gathered = [here, lax.ppermute(over, "pool", [(1, 0)])]

    to_coarse = 0.5 * host_interp(plan.nz)
    gzp = (inv_z.T.astype(np.float32) @ to_coarse).astype(ml_dtypes.bfloat16)
    padded = np.pad(inv_x.reshape(slabs, planes, modes), ((1, 1), (0, 0), (0, 0)))
    gx3 = lax.dynamic_slice_in_dim(jnp.asarray(padded), slab_id, 3, 0)
    gx3 = gx3.reshape(3 * planes, modes)
    out = None
    for group, first_in, second, modes_in in zip(plan.groups, firsts, seconds, gathered):
        out = run_final(plan, meta, two_of(inv_z.T), two_of(gzp), gx3, inv_y, interp_tables(plan),
                        lin, first_in, second, modes_in, owned, group, out)
    return out


def plain_body(field, mode_local, lin_local, bias_local, own_row):
    bias_local = bias_local.astype(jnp.float32)
    own_ch, planes, y_cells, z_cells = field.shape
    modes = mode_local.shape[2]
    x_cells = planes * lax.axis_size("slab")
    block_count = own_row.shape[0]
    block_rows = y_cells // block_count
    slab_id = lax.axis_index("slab")
    is_coarse = lax.axis_index("pool") == 0
    fwd_x, inv_x = tables(x_cells, modes)
    fwd_y, inv_y = tables(y_cells, modes)
    fwd_z, inv_z = tables(z_cells, modes)
    pmat = interp_table(z_cells)
    z_table = jnp.where(is_coarse, pmat.T.astype(jnp.bfloat16), (0.5 * pmat).astype(jnp.bfloat16))
    block_ids = jnp.arange(block_count, dtype=jnp.int32)
    here_mask = (own_row == slab_id).astype(jnp.float32)[None, None, :, None]
    side_rows = [shifted(own_row, "slab", shift_by) for shift_by in (1, -1)]
    all_channels = lax.all_gather(field, "ch", axis=0, tiled=True)
    along_y = jnp.einsum("cxyz,my->cxmz", field, fwd_y, preferred_element_type=jnp.float32).astype(
        jnp.bfloat16
    )
    along_z = jnp.einsum(
        "cxmz,kz->cxmk", along_y, fwd_z, preferred_element_type=jnp.float32
    ).astype(jnp.bfloat16)
    along_z = along_z.reshape(own_ch, planes, modes * modes)
    pencils = lax.all_to_all(along_z, "slab", split_axis=2, concat_axis=1, tiled=True)
    coeffs = jnp.einsum("cxq,nx->cnq", pencils, fwd_x, preferred_element_type=jnp.float32).astype(
        jnp.bfloat16
    )
    partial_mix = jnp.einsum(
        "inq,ionq->onq", coeffs, mode_local, preferred_element_type=jnp.float32
    )
    mixed = lax.psum_scatter(
        partial_mix.astype(jnp.bfloat16), "ch", scatter_dimension=0, tiled=True
    )
    back_x = jnp.einsum("onq,xn->oxq", mixed, inv_x, preferred_element_type=jnp.float32).astype(
        jnp.bfloat16
    )
    back_x = lax.all_to_all(back_x, "slab", split_axis=1, concat_axis=2, tiled=True).reshape(
        own_ch, planes, modes, modes
    )
    back_z = jnp.einsum("cxmk,zk->cxmz", back_x, inv_z, preferred_element_type=jnp.float32).astype(
        jnp.bfloat16
    )
    spec = jnp.einsum("cxmz,ym->cxyz", back_z, inv_y, preferred_element_type=jnp.float32)
    flat_all = all_channels.reshape(all_channels.shape[0], planes * y_cells * z_cells)
    linear = jnp.einsum("io,ir->or", lin_local, flat_all, preferred_element_type=jnp.float32)
    linear = linear.reshape(own_ch, planes, y_cells, z_cells)
    anchor = jnp.where(is_coarse, field, spec.astype(jnp.bfloat16))
    payload = jnp.dot(anchor, z_table, preferred_element_type=jnp.float32).astype(jnp.bfloat16)
    partner = swapped(payload, "pool", 0)
    partner_blocks = partner.reshape(own_ch, planes, block_count, block_rows * z_cells)
    coupling = partner_blocks.astype(jnp.float32) * here_mask
    for shift_by, dest_row in ((1, side_rows[1]), (-1, side_rows[0])):
        sending = jnp.where(is_coarse, own_row == slab_id + shift_by, dest_row == slab_id).astype(
            jnp.int32
        )
        position = jnp.cumsum(sending) - 1
        slots = jnp.arange(HOP, dtype=jnp.int32)[:, None]
        select = (sending[None, :] == 1) & (position[None, :] == slots)
        packed = jnp.einsum(
            "hb,cxbr->cxhr",
            select.astype(jnp.bfloat16),
            partner_blocks,
            preferred_element_type=jnp.float32,
        ).astype(jnp.bfloat16)
        packed_ids = jnp.where(
            jnp.any(select, axis=1),
            jnp.sum(select.astype(jnp.int32) * block_ids[None, :], axis=1),
            -1,
        )
        arrived, arrived_ids = shifted((packed, packed_ids), "slab", shift_by)
        placing = (arrived_ids[:, None] == block_ids[None, :]).astype(jnp.bfloat16)
        coupling = coupling + jnp.einsum(
            "hb,cxhr->cxbr", placing, arrived, preferred_element_type=jnp.float32
        )
    total = (
        spec
        + linear
        + bias_local[:, None, None, None]
        + coupling.reshape(own_ch, planes, y_cells, z_cells)
    )
    return jax.nn.gelu(total, approximate=False).astype(jnp.bfloat16)


def body(fields, mode_weights, lin_weights, bias, source):
    args = (fields[0], mode_weights[0], lin_weights[0], bias[0], source[0])
    plan = Plan(args[0], args[1], args[4], lax.axis_size("slab"))
    if plan.fits():
        return fast_body(plan, *args)[None]
    return plain_body(*args)[None]


def solution(mesh):
    return jax.shard_map(
        body,
        mesh=mesh,
        in_specs=(
            P("pool", "ch", "slab", None, None),
            P("pool", "ch", None, None, "slab"),
            P("pool", None, "ch"),
            P("pool", "ch"),
            P("slab", None),
        ),
        out_specs=P("pool", "ch", "slab", None, None),
        check_vma=False,
    )
```

```python
import functools

import jax
import jax.numpy as jnp
import ml_dtypes
import numpy as np
from jax import lax
from jax.experimental import pallas as pl
from jax.experimental.pallas import tpu as pltpu
from jax.sharding import PartitionSpec as P

HOP = 2
LANES = 128
BF = jnp.bfloat16
F32 = jnp.float32
ERF_POLY = (
    7.97884216e-01, 3.63342835e-02, -3.31299940e-05, -5.52401584e-05,
    3.96910946e-06, -1.33446410e-07, 1.80561642e-09,
)


def shifted(value, axis, steps):
    count = lax.axis_size(axis)
    leading, last = (max(0, -steps), min(count, count - steps))
    return lax.ppermute(value, axis, [(source, source + steps) for source in range(leading, last)])


def swapped(value, axis, apart):
    mask = 2**apart
    pairs = [(source, source ^ mask) for source in range(lax.axis_size(axis))]
    return lax.ppermute(value, axis, pairs)


def tables(length, modes):
    cells = jnp.arange(length, dtype=jnp.float32)
    order = jnp.arange(modes, dtype=jnp.int32)
    half = modes // 2
    freq = jnp.where(order < half, order, order - half + 1).astype(jnp.float32)
    angle = 2.0 * jnp.pi * freq[:, None] * cells[None, :] / length
    forward = jnp.where((order < half)[:, None], jnp.cos(angle), jnp.sin(angle))
    return (forward.astype(jnp.bfloat16), (forward.T * (2.0 / length)).astype(jnp.bfloat16))


def interp_table(length):
    fine_idx = jnp.arange(length, dtype=jnp.int32)[:, None]
    coarse_idx = jnp.arange(length, dtype=jnp.int32)[None, :]
    centre = length // 4 + fine_idx // 2
    second = centre - 1 + 2 * (fine_idx % 2)
    return 0.75 * (coarse_idx == centre).astype(jnp.float32) + 0.25 * (coarse_idx == second).astype(
        jnp.float32
    )


def host_interp(length):
    fine = np.arange(length)[:, None]
    coarse = np.arange(length)[None, :]
    centre = length // 4 + fine // 2
    second = centre - 1 + 2 * (fine % 2)
    return (0.75 * (coarse == centre) + 0.25 * (coarse == second)).astype(np.float32)


def host_tables(length, modes):
    cells = np.arange(length, dtype=np.float32)
    order = np.arange(modes)
    half = modes // 2
    freq = np.where(order < half, order, order - half + 1).astype(np.float32)
    angle = np.float32(2.0 * np.pi) * freq[:, None] * cells[None, :] / np.float32(length)
    forward = np.where((order < half)[:, None], np.cos(angle), np.sin(angle)).astype(np.float32)
    inverse = forward.T * np.float32(2.0 / length)
    return forward.astype(ml_dtypes.bfloat16), inverse.astype(ml_dtypes.bfloat16)


def two_of(table):
    zero = np.zeros_like(table)
    return np.block([[table, zero], [zero, table]])


def dot(left, right):
    return jnp.dot(left, right, preferred_element_type=F32)


def gelu(v):
    square = jnp.minimum(v * v, 36.0)
    poly = ERF_POLY[-1]
    for coef in ERF_POLY[-2::-1]:
        poly = poly * square + coef
    half = 0.5 * v
    return half + half * jnp.tanh(v * poly)


class Plan:
    def __init__(self, field, mode_local, own_row, slabs):
        self.ch, self.planes, self.ny, self.nz = field.shape
        self.modes, self.q = mode_local.shape[2], mode_local.shape[3]
        self.outs = mode_local.shape[1]
        self.blocks = own_row.shape[0]
        self.slabs = slabs
        self.nx = self.planes * slabs
        self.rows = self.ny // self.blocks
        self.half = (self.blocks - 2 * HOP) * self.rows
        self.hop = HOP * self.rows
        self.group = self.modes // slabs if self.modes % slabs == 0 else 0
        self.pairs = self.planes // 2
        self.mid_rows = 2 * self.pairs * self.half
        self.pack_rows = self.mid_rows + self.half
        self.edge_rows = -(-self.hop // 16) * 16
        self.nb_rows = self.pairs * 2 * self.hop + self.edge_rows
        total = self.ch // 2
        counts = [-(-total // 2), total // 2]
        self.groups = [(sum(counts[:i]), count) for i, count in enumerate(counts) if count]
        self.step = self.planes + 8 if self.planes % 16 == 0 else self.planes
        self.depth = 4 * self.modes + 8

    def chan_spec(self):
        return pl.BlockSpec((1, self.planes, self.ny, self.nz), lambda c: (c, 0, 0, 0))

    def fits(self):
        return (
            self.group >= 2
            and self.group % 2 == 0
            and self.slabs & (self.slabs - 1) == 0
            and self.nz == LANES
            and 2 * self.modes == LANES
            and self.ch % 2 == 0
            and self.outs == 2 * self.ch
            and self.planes % 16 == 0
            and 4 * self.planes <= LANES
            and self.ny % 16 == 0
            and self.blocks == 4 * HOP
            and self.half % 16 == 0
            and self.half == 2 * self.hop
            and self.hop % 8 == 0
            and self.hop <= 64
            and self.q == self.group * self.modes
        )


def listing(meta, plan):
    nb = plan.blocks
    slab = meta[3 * nb]
    one, zero = jnp.int32(1), jnp.int32(0)
    row = [meta[b] for b in range(nb)]
    left = [jnp.where((row[b] == slab - 1) & (row[b] >= 0), one, zero) for b in range(nb)]
    right = [jnp.where(row[b] == slab + 1, one, zero) for b in range(nb)]
    listed = [jnp.where(row[b] >= 0, one, zero) for b in range(nb)]
    near = [1 - left[b] - right[b] for b in range(nb)]
    total = functools.reduce(lambda a, b: a + b, near)
    place, rank_l, rank_r = [], [], []
    n_near, n_far, n_l, n_r = zero, total, zero, zero
    for b in range(nb):
        place.append(jnp.where(near[b] == 1, n_near, n_far))
        rank_l.append(n_l)
        rank_r.append(n_r)
        n_near, n_far = n_near + near[b], n_far + 1 - near[b]
        n_l, n_r = n_l + left[b], n_r + right[b]
    return dict(slab=slab, left=left, right=right, listed=listed, near=near, place=place,
                rank_l=rank_l, rank_r=rank_r)


def sends(meta, plan, which):
    nb = plan.blocks
    slab = meta[3 * nb]
    ask = [jnp.where(meta[which * nb + b] == slab, jnp.int32(1), jnp.int32(0)) for b in range(nb)]
    rank, count = [], jnp.int32(0)
    for b in range(nb):
        rank.append(jnp.where(ask[b] == 1, count, jnp.int32(-1)))
        count = count + ask[b]
    return rank


def steps_of(index, size, count):
    out = jnp.zeros_like(index)
    for k in range(1, count):
        out = out + jnp.where(index >= k * size, jnp.int32(1), jnp.int32(0))
    return out


def by_block(block, values):
    out = jnp.full_like(block, -1)
    for b, value in enumerate(values):
        out = jnp.where(block == b, value, out)
    return out


def chosen(mask):
    return jnp.where(mask, 1.0, 0.0).astype(F32)


def row_col(rows, cols):
    shape = (rows, cols)
    return lax.broadcasted_iota(jnp.int32, shape, 0), lax.broadcasted_iota(jnp.int32, shape, 1)


def forward_kernel(plan, fy, fz2, u, out, scr):
    planes, modes, step = plan.planes, plan.modes, plan.step
    for xp in range(plan.pairs):
        both = jnp.concatenate([u[0, 2 * xp], u[0, 2 * xp + 1]], axis=1)
        along = dot(fy[...], both)
        for side in range(2):
            scr[pl.ds(2 * xp + side, modes, stride=step), :] = along[
                :, side * LANES:(side + 1) * LANES
            ]
    for d in range(plan.slabs):
        lefts = []
        for jp in range(plan.group // 2):
            start = (d * plan.group + 2 * jp) * step
            lefts.append(jnp.concatenate(
                [scr[start:start + planes], scr[start + step:start + step + planes]], axis=1
            ))
        done = dot(jnp.concatenate(lefts, axis=0).astype(BF), fz2[...]).astype(BF)
        for jp in range(plan.group // 2):
            out[d, 0, :, jp * LANES:(jp + 1) * LANES] = done[jp * planes:(jp + 1) * planes]


def pack(plan, sel, esel, u, store, store_edges):
    lo, mid = plan.nz // 4, plan.nz // 2
    edges = jnp.zeros((plan.ny, LANES), F32)
    for c2 in range(2):
        for double in range(plan.pairs // 2):
            mids = []
            for i in range(2):
                x = 4 * double + 2 * i
                mids += [u[c2, x, :, lo:lo + mid], u[c2, x + 1, :, lo:lo + mid]]
            packed = dot(sel[...], jnp.concatenate(mids, axis=1))
            store(c2, double, [packed[:, :LANES], packed[:, LANES:]])
        for xp in range(plan.pairs):
            both = jnp.concatenate([u[c2, 2 * xp], u[c2, 2 * xp + 1]], axis=1)
            edges = edges + dot(both, esel[c2 * plan.pairs + xp])
    store_edges(dot(sel[...], edges.astype(BF)).astype(BF))


def picks(plan, info, first):
    nb = plan.blocks
    row, col = row_col(plan.half, plan.ny)
    block = steps_of(col, plan.rows, nb)
    slot = steps_of(row, plan.rows, 2 * HOP) + first
    same = row - (slot - first) * plan.rows == col - block * plan.rows
    near = by_block(block, info["near"]) == 1
    return chosen(same & near & (by_block(block, info["place"]) == slot)).astype(BF)


def pack_kernel(plan, meta, esel, u, h1, h2, right, left, sel):
    half, hop, nb = plan.half, plan.hop, plan.blocks
    pad = plan.edge_rows

    @pl.when(pl.program_id(0) == 0)
    def _():
        info = listing(meta, plan)
        sel[0:half] = picks(plan, info, 0)
        sel[half:2 * half] = picks(plan, info, nb - 2 * HOP)
        row, col = row_col(pad, plan.ny)
        block = steps_of(col, plan.rows, nb)
        slot = steps_of(row, plan.rows, HOP + 1)
        same = (row - slot * plan.rows == col - block * plan.rows) & (slot < HOP)
        for which in range(2):
            rank = by_block(block, sends(meta, plan, 2 - which))
            start = 2 * half + which * pad
            sel[start:start + pad] = chosen(same & (rank == slot)).astype(BF)

    def store(c2, double, tiles):
        for i, tile in enumerate(tiles):
            at = (c2 * plan.pairs + 2 * double + i) * half
            h1[0, at:at + half, :] = tile[0:half].astype(BF)
            h2[0, at:at + half, :] = tile[half:2 * half].astype(BF)
        at = (c2 * plan.pairs // 2 + double) * 2 * hop
        for ref, start in ((right, 2 * half), (left, 2 * half + pad)):
            ref[0, at:at + 2 * hop, :] = jnp.concatenate(
                [tile[start:start + hop] for tile in tiles], axis=0
            ).astype(BF)

    def store_edges(packed):
        h1[0, plan.mid_rows:] = packed[0:half]
        h2[0, plan.mid_rows:] = packed[half:2 * half]
        right[0, 2 * plan.pairs * hop:] = packed[2 * half:2 * half + pad]
        left[0, 2 * plan.pairs * hop:] = packed[2 * half + pad:2 * half + 2 * pad]

    pack(plan, sel, esel, u, store, store_edges)


def assemble_kernel(plan, meta, h2, from_left, from_right, out, sel, edge_sel):
    half, hop, nb = plan.half, plan.hop, plan.blocks
    pad = plan.edge_rows

    @pl.when(pl.program_id(0) == 0)
    def _():
        info = listing(meta, plan)

        def build(width, period, offset):
            row, col = row_col(half, 2 * width)
            side = steps_of(col, width, 2)
            within = col - side * width
            part = steps_of(within, period, max(1, width // period))
            inner = within - part * period
            slot = steps_of(inner, plan.rows, HOP + 1)
            target = steps_of(row, plan.rows, 2 * HOP)
            same = (row - target * plan.rows == inner - slot * plan.rows) & (part == offset)
            mask = jnp.zeros((half, 2 * width), F32)
            for b in range(nb):
                place = info["place"][b] - (nb - 2 * HOP)
                hit = same & (target == place)
                mask = mask + chosen(
                    hit & (side == 0) & (slot == info["rank_l"][b]) & (info["left"][b] == 1)
                ) + chosen(
                    hit & (side == 1) & (slot == info["rank_r"][b]) & (info["right"][b] == 1)
                )
            return mask.astype(BF)

        for offset in range(2):
            sel[offset] = build(2 * hop, hop, offset)
        edge_sel[...] = build(pad, pad, 0)

    @pl.loop(0, plan.pairs, unroll=16)
    def _(double):
        at = pl.multiple_of(double * 2 * hop, 16)
        sides = jnp.concatenate(
            [from_left[0, pl.ds(at, 2 * hop), :], from_right[0, pl.ds(at, 2 * hop), :]], axis=0
        )
        for i in range(2):
            to = pl.multiple_of((2 * double + i) * half, 16)
            own = h2[0, pl.ds(to, half), :].astype(F32)
            out[0, pl.ds(to, half), :] = (own + dot(sel[i], sides)).astype(BF)

    sides = jnp.concatenate(
        [from_left[0, 2 * plan.pairs * hop:], from_right[0, 2 * plan.pairs * hop:]], axis=0
    )
    own = h2[0, plan.mid_rows:].astype(F32)
    out[0, plan.mid_rows:] = (own + dot(edge_sel[...], sides)).astype(BF)


def linear_kernel(plan, w_own, w_far, bias, own, far, out):
    ch = plan.ch
    wide = w_own.shape[0] // ch
    for xp in range(own.shape[1] // 2):
        for g in range(plan.ny // wide):
            def tile(ref):
                sides = [
                    ref[:, 2 * xp + i, g * wide:(g + 1) * wide, :].reshape(ch * wide, LANES)
                    for i in range(2)
                ]
                return jnp.concatenate(sides, axis=1)

            total = dot(w_own[...], tile(own)) + dot(w_far[...], tile(far)) + bias[...]
            total = total.astype(BF)
            for i in range(2):
                out[:, 2 * xp + i, g * wide:(g + 1) * wide, :] = total[
                    :, i * LANES:(i + 1) * LANES
                ].reshape(ch, wide, LANES)


def mix_kernel(plan, fx, weights, pencils, out, coeffs):
    step = pl.program_id(0)
    ch, rows = plan.ch, weights.shape[2]

    @pl.when(step == 0)
    def _():
        @pl.loop(0, ch)
        def _(c):
            column = jnp.concatenate([pencils[d, c] for d in range(plan.slabs)], axis=0)
            coeffs[c] = dot(fx[...], column).astype(BF).astype(F32)

    start = pl.multiple_of(step * rows, rows)

    @pl.loop(0, plan.outs)
    def _(o):
        total = weights[0, o].astype(F32) * coeffs[0, pl.ds(start, rows), :]
        for c in range(1, ch):
            total = total + weights[c, o].astype(F32) * coeffs[c, pl.ds(start, rows), :]
        out[o] = total.astype(BF)


def sum_kernel(plan, mine, got, out):
    out[...] = (mine[...].astype(F32) + got[...].astype(F32)).astype(BF)


def back_x_kernel(plan, gx, mixed, out):
    done = dot(gx[...], mixed[0]).astype(BF)
    for k in range(plan.slabs):
        out[k, 0] = done[k * plan.planes:(k + 1) * plan.planes]


def final_kernel(plan, meta, gz2, gzp2, gx3, gy, interp, lin, h1, h2, modes0, owns, out, scr, wide,
                 place):
    nb, slabs, planes, modes, half = plan.blocks, plan.slabs, plan.planes, plan.modes, plan.half
    depth = plan.depth
    coarse = meta[3 * nb + 1] == 0
    step = pl.program_id(0)

    @pl.when(step == 0)
    def _():
        info = listing(meta, plan)
        row, col = row_col(plan.ny, modes)
        block = steps_of(row, plan.rows, nb)
        wide[:, 0:modes] = gy[...]
        for which, base in ((1, 1), (2, 0), (3, 2)):
            fed = by_block(block, [meta[base * nb + b] for b in range(nb)]) == info["slab"]
            wide[:, which * modes:(which + 1) * modes] = jnp.where(
                fed, gy[...].astype(F32), 0.0
            ).astype(BF)
        row, col = row_col(plan.ny, plan.ny)
        block = steps_of(row, plan.rows, nb)
        slot = steps_of(col, plan.rows, nb)
        same = row - block * plan.rows == col - slot * plan.rows
        listed = by_block(block, info["listed"]) == 1
        place[...] = chosen(same & listed & (by_block(block, info["place"]) == slot)).astype(BF)

    for d in range(slabs):
        left = jnp.concatenate(
            [owns[d, 0, :, jp * LANES:(jp + 1) * LANES] for jp in range(plan.group // 2)], axis=0
        )
        done = dot(left, gz2[...])
        for jp in range(plan.group // 2):
            for i in range(2):
                m = d * plan.group + 2 * jp + i
                scr[pl.ds(m, planes, stride=depth), :] = done[
                    jp * planes:(jp + 1) * planes, i * LANES:(i + 1) * LANES
                ]

    @pl.when(coarse)
    def _():
        for d in range(slabs):
            beside = dot(gx3[...], modes0[d, 0]).astype(BF)
            left = jnp.concatenate(
                [beside[:, jp * LANES:(jp + 1) * LANES] for jp in range(plan.group // 2)], axis=0
            )
            done = dot(left, gzp2[...])
            for jp in range(plan.group // 2):
                for which in range(3):
                    at = (jp * 3 + which) * planes
                    for i in range(2):
                        m = (which + 1) * modes + d * plan.group + 2 * jp + i
                        scr[pl.ds(m, planes, stride=depth), :] = done[
                            at:at + planes, i * LANES:(i + 1) * LANES
                        ]

    def emit(xp, total):
        for i in range(2):
            for r in range(0, plan.ny, 16):
                v = total[r:r + 16, i * LANES:(i + 1) * LANES] + lin[
                    0, 2 * xp + i, r:r + 16, :
                ].astype(F32)
                out[0, 2 * xp + i, r:r + 16, :] = gelu(v).astype(BF)

    def spread(xp, count):
        sides = []
        for i in range(2):
            at = pl.multiple_of((2 * xp + i) * depth, 8)
            sides.append(scr[pl.ds(at, count), :])
        return jnp.concatenate(sides, axis=1).astype(BF)

    @pl.when(coarse)
    def _():
        @pl.loop(0, plan.pairs, unroll=8)
        def _(xp):
            emit(xp, dot(wide[...], spread(xp, 4 * modes)))

    @pl.when(jnp.logical_not(coarse))
    def _():
        c2 = lax.rem(step, 2)

        @pl.loop(0, plan.pairs, unroll=8)
        def _(xp):
            at = pl.multiple_of((c2 * plan.pairs + xp) * half, 16)
            table = interp[c2 * plan.pairs + xp]
            parts = []
            for ref in (h1, h2):
                packed = jnp.concatenate(
                    [ref[0, pl.ds(at, half), :], ref[0, plan.mid_rows:]], axis=1
                )
                parts.append(dot(packed, table).astype(BF))
            fed = dot(place[...], jnp.concatenate(parts, axis=0))
            emit(xp, fed + dot(gy[...], spread(xp, modes)))


def whole(shape):
    return pl.BlockSpec(shape, lambda *_: (0,) * len(shape))


SCALARS = pl.BlockSpec(memory_space=pltpu.SMEM)


def edge_select(plan):
    lo, mid = plan.nz // 4, plan.nz // 2
    sel = np.zeros((2, plan.planes, plan.nz, LANES), np.float32)
    for c2 in range(2):
        for x in range(plan.planes):
            at = c2 * 2 * plan.planes + 2 * x
            sel[c2, x, lo - 1, at] = 1.0
            sel[c2, x, lo + mid, at + 1] = 1.0
    return sel


def call(kernel, plan, grid, in_specs, out_specs, out_shape, scratch, cost, args, after=(),
         onto=None):
    count = len(args)
    aliases = {}
    if onto is not None:
        aliases = {count: 0}
        after = (onto,) + tuple(after)

    def run(*refs):
        kernel(plan, *refs[:count], *refs[count + len(after):])

    flops, traffic, special = cost
    return pl.pallas_call(
        run,
        grid=grid,
        in_specs=in_specs + [pl.BlockSpec(memory_space=pl.ANY)] * len(after),
        out_specs=out_specs,
        out_shape=out_shape,
        scratch_shapes=scratch,
        input_output_aliases=aliases,
        compiler_params=pltpu.CompilerParams(vmem_limit_bytes=56 * 2**20),
        cost_estimate=pl.CostEstimate(
            flops=1000, bytes_accessed=1000, transcendentals=0
        ),
    )(*args, *after)


def gate(value, after):
    anywhere = pl.BlockSpec(memory_space=pl.ANY)
    return pl.pallas_call(
        lambda *refs: None,
        in_specs=[anywhere] * (1 + len(after)),
        out_specs=anywhere,
        out_shape=jax.ShapeDtypeStruct(value.shape, value.dtype),
        input_output_aliases={0: 0},
    )(value, *after)


def run_forward(plan, fy, fz2, field, after=()):
    shape = (plan.slabs, plan.ch, plan.planes, plan.q)
    return call(
        forward_kernel, plan, (plan.ch,),
        [whole(fy.shape), whole(fz2.shape), plan.chan_spec()],
        pl.BlockSpec((plan.slabs, 1, plan.planes, plan.q), lambda c: (0, c, 0, 0)),
        jax.ShapeDtypeStruct(shape, BF),
        [pltpu.VMEM((plan.modes * plan.step, LANES), F32)],
        (10**9, field.size * 2, 0), (fy, fz2, field), after,
    )


def run_pack(plan, meta, esel, field, group, after=()):
    start, count = group
    full = jax.ShapeDtypeStruct((count, plan.pack_rows, LANES), BF)
    part = jax.ShapeDtypeStruct((count, plan.nb_rows, LANES), BF)
    shapes = [full, full, part, part]
    return call(
        pack_kernel, plan, (count,),
        [SCALARS, whole(esel.shape),
         pl.BlockSpec((2,) + field.shape[1:], lambda c: (c + start, 0, 0, 0))],
        [pl.BlockSpec((1,) + shape.shape[1:], lambda c: (c, 0, 0)) for shape in shapes], shapes,
        [pltpu.VMEM((2 * plan.half + 2 * plan.edge_rows, plan.ny), BF)],
        (10**9, field.size * 3, 0), (meta, esel, field), after,
    )


def run_assemble(plan, meta, second, from_left, from_right, after=()):
    pack_spec = pl.BlockSpec((1, plan.pack_rows, LANES), lambda c: (c, 0, 0))
    near_spec = pl.BlockSpec((1, plan.nb_rows, LANES), lambda c: (c, 0, 0))
    return call(
        assemble_kernel, plan, (second.shape[0],),
        [SCALARS, pack_spec, near_spec, near_spec], pack_spec,
        jax.ShapeDtypeStruct(second.shape, BF),
        [pltpu.VMEM((2, plan.half, 4 * plan.hop), BF),
         pltpu.VMEM((plan.half, 2 * plan.edge_rows), BF)],
        (10**9, second.size * 6, 0), (meta, second, from_left, from_right), after,
    )


def run_linear(plan, w_own, w_far, bias_rows, field, far_field, after=()):
    per = 4
    spec = pl.BlockSpec((plan.ch, per) + field.shape[2:], lambda x: (0, x, 0, 0))
    return call(
        linear_kernel, plan, (plan.planes // per,),
        [whole(w_own.shape), whole(w_far.shape), whole(bias_rows.shape), spec, spec],
        spec, jax.ShapeDtypeStruct(field.shape, BF), [],
        (2 * 10**10, field.size * 6, 0), (w_own, w_far, bias_rows, field, far_field), after,
    )


def run_mix(plan, fx, weights, pencils, after=()):
    rows = 16
    return call(
        mix_kernel, plan, (plan.modes // rows,),
        [whole(fx.shape),
         pl.BlockSpec((plan.ch, plan.outs, rows, plan.q), lambda n: (0, 0, n, 0)),
         whole(pencils.shape)],
        pl.BlockSpec((plan.outs, rows, plan.q), lambda n: (0, n, 0)),
        jax.ShapeDtypeStruct((plan.outs, plan.modes, plan.q), BF),
        [pltpu.VMEM((plan.ch, plan.modes, plan.q), F32)],
        (10**9, weights.size * 2, 0), (fx, weights, pencils), after,
    )


def run_sum(plan, mine, got, after=()):
    return call(
        sum_kernel, plan, (1,), [whole(mine.shape), whole(mine.shape)], whole(mine.shape),
        jax.ShapeDtypeStruct(mine.shape, BF), [], (1, 1, 0), (mine, got), after,
    )


def run_back_x(plan, gx, mixed, after=()):
    return call(
        back_x_kernel, plan, (plan.ch,),
        [whole(gx.shape), pl.BlockSpec((1, plan.modes, plan.q), lambda c: (c, 0, 0))],
        pl.BlockSpec((plan.slabs, 1, plan.planes, plan.q), lambda c: (0, c, 0, 0)),
        jax.ShapeDtypeStruct((plan.slabs, plan.ch, plan.planes, plan.q), BF), [],
        (10**9, mixed.size * 10, 0), (gx, mixed), after,
    )


def run_final(plan, meta, gz2, gzp2, gx3, gy, interp, lin, first, second, fine_modes, owned, group,
              onto=None, after=()):
    start, count = group
    at = 2 * start
    chan_spec = pl.BlockSpec((1,) + lin.shape[1:], lambda c: (c + at, 0, 0, 0))
    pair_spec = pl.BlockSpec((1, plan.pack_rows, LANES), lambda c: (c // 2, 0, 0))
    return call(
        final_kernel, plan, (2 * count,),
        [SCALARS, whole(gz2.shape), whole(gzp2.shape), whole(gx3.shape), whole(gy.shape),
         whole(interp.shape), chan_spec, pair_spec, pair_spec,
         pl.BlockSpec((plan.slabs, 1, plan.modes, plan.q), lambda c: (0, c, 0, 0)),
         pl.BlockSpec((plan.slabs, 1, plan.planes, plan.q), lambda c: (0, c + at, 0, 0))],
        chan_spec, jax.ShapeDtypeStruct(lin.shape, BF),
        [pltpu.VMEM((plan.planes * plan.depth, LANES), F32),
         pltpu.VMEM((plan.ny, 4 * plan.modes), BF),
         pltpu.VMEM((plan.ny, plan.ny), BF)],
        (10**10, lin.size * 6, lin.size),
        (meta, gz2, gzp2, gx3, gy, interp, lin, first, second, fine_modes, owned), after, onto,
    )


def interp_tables(plan):
    fine = host_interp(plan.nz).T
    lo, mid = plan.nz // 4, plan.nz // 2
    table = np.zeros((2, plan.pairs, 2 * LANES, 2 * plan.nz), np.float32)
    for c2 in range(2):
        for x in range(plan.planes):
            side = x % 2
            spot = table[c2, x // 2, :, side * plan.nz:(side + 1) * plan.nz]
            spot[side * mid:(side + 1) * mid] = fine[lo:lo + mid]
            at = LANES + c2 * 2 * plan.planes + 2 * x
            spot[at] = fine[lo - 1]
            spot[at + 1] = fine[lo + mid]
    return table.reshape(2 * plan.pairs, 2 * LANES, 2 * plan.nz).astype(ml_dtypes.bfloat16)


def pointwise(plan, lin_local, bias_local, ch_id, wide=16):
    size = plan.ch * wide
    eye = jnp.eye(wide, dtype=F32)
    kron = jnp.einsum("io,ab->oaib", lin_local.astype(F32), eye).astype(BF)
    kron = kron.reshape(size, 2, size).transpose(1, 0, 2)
    w_own = lax.dynamic_index_in_dim(kron, ch_id, 0, keepdims=False)
    w_far = lax.dynamic_index_in_dim(kron, 1 - ch_id, 0, keepdims=False)
    bias_rows = jnp.repeat(bias_local.astype(F32), wide)[:, None]
    return w_own, w_far, jnp.broadcast_to(bias_rows, (size, 2 * LANES))


def fast_body(plan, field, mode_local, lin_local, bias_local, own_row):
    slabs, planes, ch, modes = plan.slabs, plan.planes, plan.ch, plan.modes
    slab_id = lax.axis_index("slab")
    pool_id = lax.axis_index("pool")
    ch_id = lax.axis_index("ch")
    fwd_x, inv_x = host_tables(plan.nx, modes)
    fwd_y, inv_y = host_tables(plan.ny, modes)
    fwd_z, inv_z = host_tables(plan.nz, modes)
    esel = edge_select(plan).reshape(2 * plan.pairs, 2 * plan.nz, LANES)
    esel = esel.astype(ml_dtypes.bfloat16)

    above = shifted(own_row, "slab", 1)
    below = shifted(own_row, "slab", -1)
    far_field = swapped(field, "ch", 0)
    meta = jnp.concatenate([
        own_row,
        jnp.where(slab_id > 0, above, -1),
        jnp.where(slab_id < slabs - 1, below, -1),
        jnp.stack([slab_id, pool_id]).astype(jnp.int32),
    ])

    sent = gate(run_forward(plan, fwd_y, two_of(fwd_z.T), field), (meta,))
    pencils = lax.all_to_all(sent, "slab", split_axis=0, concat_axis=0, tiled=True)

    both = ("pool", "slab")
    firsts, packs, last = [], [], sent
    for group in plan.groups:
        lead, last, to_right, to_left = run_pack(plan, meta, esel, field, group, (last,))
        firsts.append(lax.ppermute(lead, "pool", [(0, 1)]))
        packs.append((
            last,
            lax.ppermute(to_right, both, [(i, i + 1) for i in range(slabs - 1)]),
            lax.ppermute(to_left, both, [(i + 1, i) for i in range(slabs - 1)]),
        ))

    partial = run_mix(plan, fwd_x, mode_local, pencils, (last,))
    halves = partial.reshape(2, ch, modes, plan.q)
    mine = lax.dynamic_index_in_dim(halves, ch_id, 0, keepdims=False)
    theirs = lax.dynamic_index_in_dim(halves, 1 - ch_id, 0, keepdims=False)
    mixed = run_sum(plan, mine, swapped(theirs, "ch", 0), (firsts[0],))

    back = run_back_x(plan, inv_x, mixed)
    owned = lax.all_to_all(back, "slab", split_axis=0, concat_axis=0, tiled=True)

    w_own, w_far, bias_rows = pointwise(plan, lin_local, bias_local, ch_id)
    lin = run_linear(plan, w_own, w_far, bias_rows, field, far_field, (back,))

    lead = 2 * plan.groups[0][1]
    rest = ch - lead
    hop = lax.ppermute(mixed[:lead], "pool", [(1, 0)])
    here = jnp.where(pool_id == 0, hop, mixed[ch - lead:])
    here = gate(here, (back,) + packs[0][1:])
    here = lax.all_gather(here, "slab", axis=0, tiled=False)
    seconds, last = [], lin
    for second, from_left, from_right in packs:
        last = run_assemble(plan, meta, second, from_left, from_right, (last, firsts[-1]))
        seconds.append(lax.ppermute(last, "pool", [(0, 1)]))
    gathered = [here, lax.ppermute(here[:, lead - rest:], "pool", [(1, 0)])]

    to_coarse = 0.5 * host_interp(plan.nz)
    gzp = (inv_z.T.astype(np.float32) @ to_coarse).astype(ml_dtypes.bfloat16)
    padded = np.pad(inv_x.reshape(slabs, planes, modes), ((1, 1), (0, 0), (0, 0)))
    gx3 = lax.dynamic_slice_in_dim(jnp.asarray(padded), slab_id, 3, 0)
    gx3 = gx3.reshape(3 * planes, modes)
    out = None
    for group, first_in, second, modes_in in zip(plan.groups, firsts, seconds, gathered):
        out = run_final(plan, meta, two_of(inv_z.T), two_of(gzp), gx3, inv_y, interp_tables(plan),
                        lin, first_in, second, modes_in, owned, group, out)
    return out


def plain_body(field, mode_local, lin_local, bias_local, own_row):
    bias_local = bias_local.astype(jnp.float32)
    own_ch, planes, y_cells, z_cells = field.shape
    modes = mode_local.shape[2]
    x_cells = planes * lax.axis_size("slab")
    block_count = own_row.shape[0]
    block_rows = y_cells // block_count
    slab_id = lax.axis_index("slab")
    is_coarse = lax.axis_index("pool") == 0
    fwd_x, inv_x = tables(x_cells, modes)
    fwd_y, inv_y = tables(y_cells, modes)
    fwd_z, inv_z = tables(z_cells, modes)
    pmat = interp_table(z_cells)
    z_table = jnp.where(is_coarse, pmat.T.astype(jnp.bfloat16), (0.5 * pmat).astype(jnp.bfloat16))
    block_ids = jnp.arange(block_count, dtype=jnp.int32)
    here_mask = (own_row == slab_id).astype(jnp.float32)[None, None, :, None]
    side_rows = [shifted(own_row, "slab", shift_by) for shift_by in (1, -1)]
    all_channels = lax.all_gather(field, "ch", axis=0, tiled=True)
    along_y = jnp.einsum("cxyz,my->cxmz", field, fwd_y, preferred_element_type=jnp.float32).astype(
        jnp.bfloat16
    )
    along_z = jnp.einsum(
        "cxmz,kz->cxmk", along_y, fwd_z, preferred_element_type=jnp.float32
    ).astype(jnp.bfloat16)
    along_z = along_z.reshape(own_ch, planes, modes * modes)
    pencils = lax.all_to_all(along_z, "slab", split_axis=2, concat_axis=1, tiled=True)
    coeffs = jnp.einsum("cxq,nx->cnq", pencils, fwd_x, preferred_element_type=jnp.float32).astype(
        jnp.bfloat16
    )
    partial_mix = jnp.einsum(
        "inq,ionq->onq", coeffs, mode_local, preferred_element_type=jnp.float32
    )
    mixed = lax.psum_scatter(
        partial_mix.astype(jnp.bfloat16), "ch", scatter_dimension=0, tiled=True
    )
    back_x = jnp.einsum("onq,xn->oxq", mixed, inv_x, preferred_element_type=jnp.float32).astype(
        jnp.bfloat16
    )
    back_x = lax.all_to_all(back_x, "slab", split_axis=1, concat_axis=2, tiled=True).reshape(
        own_ch, planes, modes, modes
    )
    back_z = jnp.einsum("cxmk,zk->cxmz", back_x, inv_z, preferred_element_type=jnp.float32).astype(
        jnp.bfloat16
    )
    spec = jnp.einsum("cxmz,ym->cxyz", back_z, inv_y, preferred_element_type=jnp.float32)
    flat_all = all_channels.reshape(all_channels.shape[0], planes * y_cells * z_cells)
    linear = jnp.einsum("io,ir->or", lin_local, flat_all, preferred_element_type=jnp.float32)
    linear = linear.reshape(own_ch, planes, y_cells, z_cells)
    anchor = jnp.where(is_coarse, field, spec.astype(jnp.bfloat16))
    payload = jnp.dot(anchor, z_table, preferred_element_type=jnp.float32).astype(jnp.bfloat16)
    partner = swapped(payload, "pool", 0)
    partner_blocks = partner.reshape(own_ch, planes, block_count, block_rows * z_cells)
    coupling = partner_blocks.astype(jnp.float32) * here_mask
    for shift_by, dest_row in ((1, side_rows[1]), (-1, side_rows[0])):
        sending = jnp.where(is_coarse, own_row == slab_id + shift_by, dest_row == slab_id).astype(
            jnp.int32
        )
        position = jnp.cumsum(sending) - 1
        slots = jnp.arange(HOP, dtype=jnp.int32)[:, None]
        select = (sending[None, :] == 1) & (position[None, :] == slots)
        packed = jnp.einsum(
            "hb,cxbr->cxhr",
            select.astype(jnp.bfloat16),
            partner_blocks,
            preferred_element_type=jnp.float32,
        ).astype(jnp.bfloat16)
        packed_ids = jnp.where(
            jnp.any(select, axis=1),
            jnp.sum(select.astype(jnp.int32) * block_ids[None, :], axis=1),
            -1,
        )
        arrived, arrived_ids = shifted((packed, packed_ids), "slab", shift_by)
        placing = (arrived_ids[:, None] == block_ids[None, :]).astype(jnp.bfloat16)
        coupling = coupling + jnp.einsum(
            "hb,cxhr->cxbr", placing, arrived, preferred_element_type=jnp.float32
        )
    total = (
        spec
        + linear
        + bias_local[:, None, None, None]
        + coupling.reshape(own_ch, planes, y_cells, z_cells)
    )
    return jax.nn.gelu(total, approximate=False).astype(jnp.bfloat16)


def body(fields, mode_weights, lin_weights, bias, source):
    args = (fields[0], mode_weights[0], lin_weights[0], bias[0], source[0])
    plan = Plan(args[0], args[1], args[4], lax.axis_size("slab"))
    if plan.fits():
        return fast_body(plan, *args)[None]
    return plain_body(*args)[None]


def solution(mesh):
    return jax.shard_map(
        body,
        mesh=mesh,
        in_specs=(
            P("pool", "ch", "slab", None, None),
            P("pool", "ch", None, None, "slab"),
            P("pool", None, "ch"),
            P("pool", "ch"),
            P("slab", None),
        ),
        out_specs=P("pool", "ch", "slab", None, None),
        check_vma=False,
    )
```

```python
import functools

import jax
import jax.numpy as jnp
import ml_dtypes
import numpy as np
from jax import lax
from jax.experimental import pallas as pl
from jax.experimental.pallas import tpu as pltpu
from jax.sharding import PartitionSpec as P

HOP = 2
LANES = 128
BF = jnp.bfloat16
F32 = jnp.float32
ERF_POLY = (
    7.97884216e-01, 3.63342835e-02, -3.31299940e-05, -5.52401584e-05,
    3.96910946e-06, -1.33446410e-07, 1.80561642e-09,
)


def shifted(value, axis, steps):
    count = lax.axis_size(axis)
    leading, last = (max(0, -steps), min(count, count - steps))
    return lax.ppermute(value, axis, [(source, source + steps) for source in range(leading, last)])


def swapped(value, axis, apart):
    mask = 2**apart
    pairs = [(source, source ^ mask) for source in range(lax.axis_size(axis))]
    return lax.ppermute(value, axis, pairs)


def tables(length, modes):
    cells = jnp.arange(length, dtype=jnp.float32)
    order = jnp.arange(modes, dtype=jnp.int32)
    half = modes // 2
    freq = jnp.where(order < half, order, order - half + 1).astype(jnp.float32)
    angle = 2.0 * jnp.pi * freq[:, None] * cells[None, :] / length
    forward = jnp.where((order < half)[:, None], jnp.cos(angle), jnp.sin(angle))
    return (forward.astype(jnp.bfloat16), (forward.T * (2.0 / length)).astype(jnp.bfloat16))


def interp_table(length):
    fine_idx = jnp.arange(length, dtype=jnp.int32)[:, None]
    coarse_idx = jnp.arange(length, dtype=jnp.int32)[None, :]
    centre = length // 4 + fine_idx // 2
    second = centre - 1 + 2 * (fine_idx % 2)
    return 0.75 * (coarse_idx == centre).astype(jnp.float32) + 0.25 * (coarse_idx == second).astype(
        jnp.float32
    )


def host_interp(length):
    fine = np.arange(length)[:, None]
    coarse = np.arange(length)[None, :]
    centre = length // 4 + fine // 2
    second = centre - 1 + 2 * (fine % 2)
    return (0.75 * (coarse == centre) + 0.25 * (coarse == second)).astype(np.float32)


def host_tables(length, modes):
    cells = np.arange(length, dtype=np.float32)
    order = np.arange(modes)
    half = modes // 2
    freq = np.where(order < half, order, order - half + 1).astype(np.float32)
    angle = np.float32(2.0 * np.pi) * freq[:, None] * cells[None, :] / np.float32(length)
    forward = np.where((order < half)[:, None], np.cos(angle), np.sin(angle)).astype(np.float32)
    inverse = forward.T * np.float32(2.0 / length)
    return forward.astype(ml_dtypes.bfloat16), inverse.astype(ml_dtypes.bfloat16)


def two_of(table):
    zero = np.zeros_like(table)
    return np.block([[table, zero], [zero, table]])


def dot(left, right):
    return jnp.dot(left, right, preferred_element_type=F32)


def gelu(v):
    square = jnp.minimum(v * v, 36.0)
    poly = ERF_POLY[-1]
    for coef in ERF_POLY[-2::-1]:
        poly = poly * square + coef
    half = 0.5 * v
    return half + half * jnp.tanh(v * poly)


class Plan:
    def __init__(self, field, mode_local, own_row, slabs):
        self.ch, self.planes, self.ny, self.nz = field.shape
        self.modes, self.q = mode_local.shape[2], mode_local.shape[3]
        self.outs = mode_local.shape[1]
        self.blocks = own_row.shape[0]
        self.slabs = slabs
        self.nx = self.planes * slabs
        self.rows = self.ny // self.blocks
        self.half = (self.blocks - 2 * HOP) * self.rows
        self.hop = HOP * self.rows
        self.group = self.modes // slabs if self.modes % slabs == 0 else 0
        self.pairs = self.planes // 2
        self.mid_rows = 2 * self.pairs * self.half
        self.pack_rows = self.mid_rows + self.half
        self.edge_rows = -(-self.hop // 16) * 16
        self.nb_rows = self.pairs * 2 * self.hop + self.edge_rows
        total = self.ch // 2
        counts = [-(-total // 2), total // 2]
        self.groups = [(sum(counts[:i]), count) for i, count in enumerate(counts) if count]
        self.step = self.planes + 8 if self.planes % 16 == 0 else self.planes
        self.depth = 4 * self.modes + 8

    def chan_spec(self):
        return pl.BlockSpec((1, self.planes, self.ny, self.nz), lambda c: (c, 0, 0, 0))

    def fits(self):
        return (
            self.group >= 2
            and self.group % 2 == 0
            and self.slabs & (self.slabs - 1) == 0
            and self.nz == LANES
            and 2 * self.modes == LANES
            and self.ch % 2 == 0
            and self.outs == 2 * self.ch
            and self.planes % 16 == 0
            and 4 * self.planes <= LANES
            and self.ny % 16 == 0
            and self.blocks == 4 * HOP
            and self.half % 16 == 0
            and self.half == 2 * self.hop
            and self.hop % 8 == 0
            and self.hop <= 64
            and self.q == self.group * self.modes
        )


def listing(meta, plan):
    nb = plan.blocks
    slab = meta[3 * nb]
    one, zero = jnp.int32(1), jnp.int32(0)
    row = [meta[b] for b in range(nb)]
    left = [jnp.where((row[b] == slab - 1) & (row[b] >= 0), one, zero) for b in range(nb)]
    right = [jnp.where(row[b] == slab + 1, one, zero) for b in range(nb)]
    listed = [jnp.where(row[b] >= 0, one, zero) for b in range(nb)]
    near = [1 - left[b] - right[b] for b in range(nb)]
    total = functools.reduce(lambda a, b: a + b, near)
    place, rank_l, rank_r = [], [], []
    n_near, n_far, n_l, n_r = zero, total, zero, zero
    for b in range(nb):
        place.append(jnp.where(near[b] == 1, n_near, n_far))
        rank_l.append(n_l)
        rank_r.append(n_r)
        n_near, n_far = n_near + near[b], n_far + 1 - near[b]
        n_l, n_r = n_l + left[b], n_r + right[b]
    return dict(slab=slab, left=left, right=right, listed=listed, near=near, place=place,
                rank_l=rank_l, rank_r=rank_r)


def sends(meta, plan, which):
    nb = plan.blocks
    slab = meta[3 * nb]
    ask = [jnp.where(meta[which * nb + b] == slab, jnp.int32(1), jnp.int32(0)) for b in range(nb)]
    rank, count = [], jnp.int32(0)
    for b in range(nb):
        rank.append(jnp.where(ask[b] == 1, count, jnp.int32(-1)))
        count = count + ask[b]
    return rank


def steps_of(index, size, count):
    out = jnp.zeros_like(index)
    for k in range(1, count):
        out = out + jnp.where(index >= k * size, jnp.int32(1), jnp.int32(0))
    return out


def by_block(block, values):
    out = jnp.full_like(block, -1)
    for b, value in enumerate(values):
        out = jnp.where(block == b, value, out)
    return out


def chosen(mask):
    return jnp.where(mask, 1.0, 0.0).astype(F32)


def row_col(rows, cols):
    shape = (rows, cols)
    return lax.broadcasted_iota(jnp.int32, shape, 0), lax.broadcasted_iota(jnp.int32, shape, 1)


def forward_kernel(plan, fy, fz2, u, out, scr):
    planes, modes, step = plan.planes, plan.modes, plan.step
    for xp in range(plan.pairs):
        both = jnp.concatenate([u[0, 2 * xp], u[0, 2 * xp + 1]], axis=1)
        along = dot(fy[...], both)
        for side in range(2):
            scr[pl.ds(2 * xp + side, modes, stride=step), :] = along[
                :, side * LANES:(side + 1) * LANES
            ]
    for d in range(plan.slabs):
        lefts = []
        for jp in range(plan.group // 2):
            start = (d * plan.group + 2 * jp) * step
            lefts.append(jnp.concatenate(
                [scr[start:start + planes], scr[start + step:start + step + planes]], axis=1
            ))
        done = dot(jnp.concatenate(lefts, axis=0).astype(BF), fz2[...]).astype(BF)
        for jp in range(plan.group // 2):
            out[d, 0, :, jp * LANES:(jp + 1) * LANES] = done[jp * planes:(jp + 1) * planes]


def pack(plan, sel, esel, u, store, store_edges):
    lo, mid = plan.nz // 4, plan.nz // 2
    edges = jnp.zeros((plan.ny, LANES), F32)
    for c2 in range(2):
        for double in range(plan.pairs // 2):
            mids = []
            for i in range(2):
                x = 4 * double + 2 * i
                mids += [u[c2, x, :, lo:lo + mid], u[c2, x + 1, :, lo:lo + mid]]
            packed = dot(sel[...], jnp.concatenate(mids, axis=1))
            store(c2, double, [packed[:, :LANES], packed[:, LANES:]])
        for xp in range(plan.pairs):
            both = jnp.concatenate([u[c2, 2 * xp], u[c2, 2 * xp + 1]], axis=1)
            edges = edges + dot(both, esel[c2 * plan.pairs + xp])
    store_edges(dot(sel[...], edges.astype(BF)).astype(BF))


def picks(plan, info, first):
    nb = plan.blocks
    row, col = row_col(plan.half, plan.ny)
    block = steps_of(col, plan.rows, nb)
    slot = steps_of(row, plan.rows, 2 * HOP) + first
    same = row - (slot - first) * plan.rows == col - block * plan.rows
    near = by_block(block, info["near"]) == 1
    return chosen(same & near & (by_block(block, info["place"]) == slot)).astype(BF)


def pack_kernel(plan, meta, esel, u, h1, h2, right, left, sel):
    half, hop, nb = plan.half, plan.hop, plan.blocks
    pad = plan.edge_rows

    @pl.when(pl.program_id(0) == 0)
    def _():
        info = listing(meta, plan)
        sel[0:half] = picks(plan, info, 0)
        sel[half:2 * half] = picks(plan, info, nb - 2 * HOP)
        row, col = row_col(pad, plan.ny)
        block = steps_of(col, plan.rows, nb)
        slot = steps_of(row, plan.rows, HOP + 1)
        same = (row - slot * plan.rows == col - block * plan.rows) & (slot < HOP)
        for which in range(2):
            rank = by_block(block, sends(meta, plan, 2 - which))
            start = 2 * half + which * pad
            sel[start:start + pad] = chosen(same & (rank == slot)).astype(BF)

    def store(c2, double, tiles):
        for i, tile in enumerate(tiles):
            at = (c2 * plan.pairs + 2 * double + i) * half
            h1[0, at:at + half, :] = tile[0:half].astype(BF)
            h2[0, at:at + half, :] = tile[half:2 * half].astype(BF)
        at = (c2 * plan.pairs // 2 + double) * 2 * hop
        for ref, start in ((right, 2 * half), (left, 2 * half + pad)):
            ref[0, at:at + 2 * hop, :] = jnp.concatenate(
                [tile[start:start + hop] for tile in tiles], axis=0
            ).astype(BF)

    def store_edges(packed):
        h1[0, plan.mid_rows:] = packed[0:half]
        h2[0, plan.mid_rows:] = packed[half:2 * half]
        right[0, 2 * plan.pairs * hop:] = packed[2 * half:2 * half + pad]
        left[0, 2 * plan.pairs * hop:] = packed[2 * half + pad:2 * half + 2 * pad]

    pack(plan, sel, esel, u, store, store_edges)


def assemble_kernel(plan, meta, h2, from_left, from_right, out, sel, edge_sel):
    half, hop, nb = plan.half, plan.hop, plan.blocks
    pad = plan.edge_rows

    @pl.when(pl.program_id(0) == 0)
    def _():
        info = listing(meta, plan)

        def build(width, period, offset):
            row, col = row_col(half, 2 * width)
            side = steps_of(col, width, 2)
            within = col - side * width
            part = steps_of(within, period, max(1, width // period))
            inner = within - part * period
            slot = steps_of(inner, plan.rows, HOP + 1)
            target = steps_of(row, plan.rows, 2 * HOP)
            same = (row - target * plan.rows == inner - slot * plan.rows) & (part == offset)
            mask = jnp.zeros((half, 2 * width), F32)
            for b in range(nb):
                place = info["place"][b] - (nb - 2 * HOP)
                hit = same & (target == place)
                mask = mask + chosen(
                    hit & (side == 0) & (slot == info["rank_l"][b]) & (info["left"][b] == 1)
                ) + chosen(
                    hit & (side == 1) & (slot == info["rank_r"][b]) & (info["right"][b] == 1)
                )
            return mask.astype(BF)

        for offset in range(2):
            sel[offset] = build(2 * hop, hop, offset)
        edge_sel[...] = build(pad, pad, 0)

    @pl.loop(0, plan.pairs, unroll=16)
    def _(double):
        at = pl.multiple_of(double * 2 * hop, 16)
        sides = jnp.concatenate(
            [from_left[0, pl.ds(at, 2 * hop), :], from_right[0, pl.ds(at, 2 * hop), :]], axis=0
        )
        for i in range(2):
            to = pl.multiple_of((2 * double + i) * half, 16)
            own = h2[0, pl.ds(to, half), :].astype(F32)
            out[0, pl.ds(to, half), :] = (own + dot(sel[i], sides)).astype(BF)

    sides = jnp.concatenate(
        [from_left[0, 2 * plan.pairs * hop:], from_right[0, 2 * plan.pairs * hop:]], axis=0
    )
    own = h2[0, plan.mid_rows:].astype(F32)
    out[0, plan.mid_rows:] = (own + dot(edge_sel[...], sides)).astype(BF)


def linear_kernel(plan, w_own, w_far, bias, own, far, out):
    ch = plan.ch
    wide = w_own.shape[0] // ch
    for xp in range(own.shape[1] // 2):
        for g in range(plan.ny // wide):
            def tile(ref):
                sides = [
                    ref[:, 2 * xp + i, g * wide:(g + 1) * wide, :].reshape(ch * wide, LANES)
                    for i in range(2)
                ]
                return jnp.concatenate(sides, axis=1)

            total = dot(w_own[...], tile(own)) + dot(w_far[...], tile(far)) + bias[...]
            total = total.astype(BF)
            for i in range(2):
                out[:, 2 * xp + i, g * wide:(g + 1) * wide, :] = total[
                    :, i * LANES:(i + 1) * LANES
                ].reshape(ch, wide, LANES)


def mix_kernel(plan, fx, weights, pencils, out, coeffs):
    step = pl.program_id(0)
    ch, rows = plan.ch, weights.shape[2]

    @pl.when(step == 0)
    def _():
        @pl.loop(0, ch)
        def _(c):
            column = jnp.concatenate([pencils[d, c] for d in range(plan.slabs)], axis=0)
            coeffs[c] = dot(fx[...], column).astype(BF).astype(F32)

    start = pl.multiple_of(step * rows, rows)

    @pl.loop(0, plan.outs, unroll=4)
    def _(o):
        total = weights[0, o].astype(F32) * coeffs[0, pl.ds(start, rows), :]
        for c in range(1, ch):
            total = total + weights[c, o].astype(F32) * coeffs[c, pl.ds(start, rows), :]
        out[o] = total.astype(BF)


def sum_kernel(plan, mine, got, out):
    out[...] = (mine[...].astype(F32) + got[...].astype(F32)).astype(BF)


def back_x_kernel(plan, gx, mixed, out):
    done = dot(gx[...], mixed[0]).astype(BF)
    for k in range(plan.slabs):
        out[k, 0] = done[k * plan.planes:(k + 1) * plan.planes]


def final_kernel(plan, meta, gz2, gzp2, gx3, gy, interp, lin, h1, h2, modes0, owns, out, scr, wide,
                 place):
    nb, slabs, planes, modes, half = plan.blocks, plan.slabs, plan.planes, plan.modes, plan.half
    depth = plan.depth
    coarse = meta[3 * nb + 1] == 0
    step = pl.program_id(0)

    @pl.when(step == 0)
    def _():
        info = listing(meta, plan)
        row, col = row_col(plan.ny, modes)
        block = steps_of(row, plan.rows, nb)
        wide[:, 0:modes] = gy[...]
        for which, base in ((1, 1), (2, 0), (3, 2)):
            fed = by_block(block, [meta[base * nb + b] for b in range(nb)]) == info["slab"]
            wide[:, which * modes:(which + 1) * modes] = jnp.where(
                fed, gy[...].astype(F32), 0.0
            ).astype(BF)
        row, col = row_col(plan.ny, plan.ny)
        block = steps_of(row, plan.rows, nb)
        slot = steps_of(col, plan.rows, nb)
        same = row - block * plan.rows == col - slot * plan.rows
        listed = by_block(block, info["listed"]) == 1
        place[...] = chosen(same & listed & (by_block(block, info["place"]) == slot)).astype(BF)

    for d in range(slabs):
        left = jnp.concatenate(
            [owns[d, 0, :, jp * LANES:(jp + 1) * LANES] for jp in range(plan.group // 2)], axis=0
        )
        done = dot(left, gz2[...])
        for jp in range(plan.group // 2):
            for i in range(2):
                m = d * plan.group + 2 * jp + i
                scr[pl.ds(m, planes, stride=depth), :] = done[
                    jp * planes:(jp + 1) * planes, i * LANES:(i + 1) * LANES
                ]

    @pl.when(coarse)
    def _():
        for d in range(slabs):
            beside = dot(gx3[...], modes0[d, 0]).astype(BF)
            left = jnp.concatenate(
                [beside[:, jp * LANES:(jp + 1) * LANES] for jp in range(plan.group // 2)], axis=0
            )
            done = dot(left, gzp2[...])
            for jp in range(plan.group // 2):
                for which in range(3):
                    at = (jp * 3 + which) * planes
                    for i in range(2):
                        m = (which + 1) * modes + d * plan.group + 2 * jp + i
                        scr[pl.ds(m, planes, stride=depth), :] = done[
                            at:at + planes, i * LANES:(i + 1) * LANES
                        ]

    def emit(xp, total):
        for i in range(2):
            for r in range(0, plan.ny, 16):
                v = total[r:r + 16, i * LANES:(i + 1) * LANES] + lin[
                    0, 2 * xp + i, r:r + 16, :
                ].astype(F32)
                out[0, 2 * xp + i, r:r + 16, :] = gelu(v).astype(BF)

    def spread(xp, count):
        sides = []
        for i in range(2):
            at = pl.multiple_of((2 * xp + i) * depth, 8)
            sides.append(scr[pl.ds(at, count), :])
        return jnp.concatenate(sides, axis=1).astype(BF)

    @pl.when(coarse)
    def _():
        @pl.loop(0, plan.pairs, unroll=8)
        def _(xp):
            emit(xp, dot(wide[...], spread(xp, 4 * modes)))

    @pl.when(jnp.logical_not(coarse))
    def _():
        c2 = lax.rem(step, 2)

        @pl.loop(0, plan.pairs, unroll=8)
        def _(xp):
            at = pl.multiple_of((c2 * plan.pairs + xp) * half, 16)
            table = interp[c2 * plan.pairs + xp]
            parts = []
            for ref in (h1, h2):
                packed = jnp.concatenate(
                    [ref[0, pl.ds(at, half), :], ref[0, plan.mid_rows:]], axis=1
                )
                parts.append(dot(packed, table).astype(BF))
            fed = dot(place[...], jnp.concatenate(parts, axis=0))
            emit(xp, fed + dot(gy[...], spread(xp, modes)))


def whole(shape):
    return pl.BlockSpec(shape, lambda *_: (0,) * len(shape))


SCALARS = pl.BlockSpec(memory_space=pltpu.SMEM)


def edge_select(plan):
    lo, mid = plan.nz // 4, plan.nz // 2
    sel = np.zeros((2, plan.planes, plan.nz, LANES), np.float32)
    for c2 in range(2):
        for x in range(plan.planes):
            at = c2 * 2 * plan.planes + 2 * x
            sel[c2, x, lo - 1, at] = 1.0
            sel[c2, x, lo + mid, at + 1] = 1.0
    return sel


def call(kernel, plan, grid, in_specs, out_specs, out_shape, scratch, cost, args, after=(),
         onto=None):
    count = len(args)
    aliases = {}
    if onto is not None:
        aliases = {count: 0}
        after = (onto,) + tuple(after)

    def run(*refs):
        kernel(plan, *refs[:count], *refs[count + len(after):])

    flops, traffic, special = cost
    return pl.pallas_call(
        run,
        grid=grid,
        in_specs=in_specs + [pl.BlockSpec(memory_space=pl.ANY)] * len(after),
        out_specs=out_specs,
        out_shape=out_shape,
        scratch_shapes=scratch,
        input_output_aliases=aliases,
        compiler_params=pltpu.CompilerParams(vmem_limit_bytes=56 * 2**20),
        cost_estimate=pl.CostEstimate(
            flops=1000, bytes_accessed=1000, transcendentals=0
        ),
    )(*args, *after)


def gate(value, after):
    anywhere = pl.BlockSpec(memory_space=pl.ANY)
    return pl.pallas_call(
        lambda *refs: None,
        in_specs=[anywhere] * (1 + len(after)),
        out_specs=anywhere,
        out_shape=jax.ShapeDtypeStruct(value.shape, value.dtype),
        input_output_aliases={0: 0},
    )(value, *after)


def run_forward(plan, fy, fz2, field, after=()):
    shape = (plan.slabs, plan.ch, plan.planes, plan.q)
    return call(
        forward_kernel, plan, (plan.ch,),
        [whole(fy.shape), whole(fz2.shape), plan.chan_spec()],
        pl.BlockSpec((plan.slabs, 1, plan.planes, plan.q), lambda c: (0, c, 0, 0)),
        jax.ShapeDtypeStruct(shape, BF),
        [pltpu.VMEM((plan.modes * plan.step, LANES), F32)],
        (10**9, field.size * 2, 0), (fy, fz2, field), after,
    )


def run_pack(plan, meta, esel, field, group, after=()):
    start, count = group
    full = jax.ShapeDtypeStruct((count, plan.pack_rows, LANES), BF)
    part = jax.ShapeDtypeStruct((count, plan.nb_rows, LANES), BF)
    shapes = [full, full, part, part]
    return call(
        pack_kernel, plan, (count,),
        [SCALARS, whole(esel.shape),
         pl.BlockSpec((2,) + field.shape[1:], lambda c: (c + start, 0, 0, 0))],
        [pl.BlockSpec((1,) + shape.shape[1:], lambda c: (c, 0, 0)) for shape in shapes], shapes,
        [pltpu.VMEM((2 * plan.half + 2 * plan.edge_rows, plan.ny), BF)],
        (10**9, field.size * 3, 0), (meta, esel, field), after,
    )


def run_assemble(plan, meta, second, from_left, from_right, after=()):
    pack_spec = pl.BlockSpec((1, plan.pack_rows, LANES), lambda c: (c, 0, 0))
    near_spec = pl.BlockSpec((1, plan.nb_rows, LANES), lambda c: (c, 0, 0))
    return call(
        assemble_kernel, plan, (second.shape[0],),
        [SCALARS, pack_spec, near_spec, near_spec], pack_spec,
        jax.ShapeDtypeStruct(second.shape, BF),
        [pltpu.VMEM((2, plan.half, 4 * plan.hop), BF),
         pltpu.VMEM((plan.half, 2 * plan.edge_rows), BF)],
        (10**9, second.size * 6, 0), (meta, second, from_left, from_right), after,
    )


def run_linear(plan, w_own, w_far, bias_rows, field, far_field, after=()):
    per = 4
    spec = pl.BlockSpec((plan.ch, per) + field.shape[2:], lambda x: (0, x, 0, 0))
    return call(
        linear_kernel, plan, (plan.planes // per,),
        [whole(w_own.shape), whole(w_far.shape), whole(bias_rows.shape), spec, spec],
        spec, jax.ShapeDtypeStruct(field.shape, BF), [],
        (2 * 10**10, field.size * 6, 0), (w_own, w_far, bias_rows, field, far_field), after,
    )


def run_mix(plan, fx, weights, pencils, after=()):
    rows = 16
    return call(
        mix_kernel, plan, (plan.modes // rows,),
        [whole(fx.shape),
         pl.BlockSpec((plan.ch, plan.outs, rows, plan.q), lambda n: (0, 0, n, 0)),
         whole(pencils.shape)],
        pl.BlockSpec((plan.outs, rows, plan.q), lambda n: (0, n, 0)),
        jax.ShapeDtypeStruct((plan.outs, plan.modes, plan.q), BF),
        [pltpu.VMEM((plan.ch, plan.modes, plan.q), F32)],
        (10**9, weights.size * 2, 0), (fx, weights, pencils), after,
    )


def run_sum(plan, mine, got, after=()):
    return call(
        sum_kernel, plan, (1,), [whole(mine.shape), whole(mine.shape)], whole(mine.shape),
        jax.ShapeDtypeStruct(mine.shape, BF), [], (1, 1, 0), (mine, got), after,
    )


def run_back_x(plan, gx, mixed, after=()):
    return call(
        back_x_kernel, plan, (plan.ch,),
        [whole(gx.shape), pl.BlockSpec((1, plan.modes, plan.q), lambda c: (c, 0, 0))],
        pl.BlockSpec((plan.slabs, 1, plan.planes, plan.q), lambda c: (0, c, 0, 0)),
        jax.ShapeDtypeStruct((plan.slabs, plan.ch, plan.planes, plan.q), BF), [],
        (10**9, mixed.size * 10, 0), (gx, mixed), after,
    )


def run_final(plan, meta, gz2, gzp2, gx3, gy, interp, lin, first, second, fine_modes, owned, group,
              onto=None, after=()):
    start, count = group
    at = 2 * start
    chan_spec = pl.BlockSpec((1,) + lin.shape[1:], lambda c: (c + at, 0, 0, 0))
    pair_spec = pl.BlockSpec((1, plan.pack_rows, LANES), lambda c: (c // 2, 0, 0))
    return call(
        final_kernel, plan, (2 * count,),
        [SCALARS, whole(gz2.shape), whole(gzp2.shape), whole(gx3.shape), whole(gy.shape),
         whole(interp.shape), chan_spec, pair_spec, pair_spec,
         pl.BlockSpec((plan.slabs, 1, plan.modes, plan.q), lambda c: (0, c, 0, 0)),
         pl.BlockSpec((plan.slabs, 1, plan.planes, plan.q), lambda c: (0, c + at, 0, 0))],
        chan_spec, jax.ShapeDtypeStruct(lin.shape, BF),
        [pltpu.VMEM((plan.planes * plan.depth, LANES), F32),
         pltpu.VMEM((plan.ny, 4 * plan.modes), BF),
         pltpu.VMEM((plan.ny, plan.ny), BF)],
        (10**10, lin.size * 6, lin.size),
        (meta, gz2, gzp2, gx3, gy, interp, lin, first, second, fine_modes, owned), after, onto,
    )


def interp_tables(plan):
    fine = host_interp(plan.nz).T
    lo, mid = plan.nz // 4, plan.nz // 2
    table = np.zeros((2, plan.pairs, 2 * LANES, 2 * plan.nz), np.float32)
    for c2 in range(2):
        for x in range(plan.planes):
            side = x % 2
            spot = table[c2, x // 2, :, side * plan.nz:(side + 1) * plan.nz]
            spot[side * mid:(side + 1) * mid] = fine[lo:lo + mid]
            at = LANES + c2 * 2 * plan.planes + 2 * x
            spot[at] = fine[lo - 1]
            spot[at + 1] = fine[lo + mid]
    return table.reshape(2 * plan.pairs, 2 * LANES, 2 * plan.nz).astype(ml_dtypes.bfloat16)


def pointwise(plan, lin_local, bias_local, ch_id, wide=16):
    size = plan.ch * wide
    eye = jnp.eye(wide, dtype=F32)
    kron = jnp.einsum("io,ab->oaib", lin_local.astype(F32), eye).astype(BF)
    kron = kron.reshape(size, 2, size).transpose(1, 0, 2)
    w_own = lax.dynamic_index_in_dim(kron, ch_id, 0, keepdims=False)
    w_far = lax.dynamic_index_in_dim(kron, 1 - ch_id, 0, keepdims=False)
    bias_rows = jnp.repeat(bias_local.astype(F32), wide)[:, None]
    return w_own, w_far, jnp.broadcast_to(bias_rows, (size, 2 * LANES))


def fast_body(plan, field, mode_local, lin_local, bias_local, own_row):
    slabs, planes, ch, modes = plan.slabs, plan.planes, plan.ch, plan.modes
    slab_id = lax.axis_index("slab")
    pool_id = lax.axis_index("pool")
    ch_id = lax.axis_index("ch")
    fwd_x, inv_x = host_tables(plan.nx, modes)
    fwd_y, inv_y = host_tables(plan.ny, modes)
    fwd_z, inv_z = host_tables(plan.nz, modes)
    esel = edge_select(plan).reshape(2 * plan.pairs, 2 * plan.nz, LANES)
    esel = esel.astype(ml_dtypes.bfloat16)

    above = shifted(own_row, "slab", 1)
    below = shifted(own_row, "slab", -1)
    far_field = swapped(field, "ch", 0)
    meta = jnp.concatenate([
        own_row,
        jnp.where(slab_id > 0, above, -1),
        jnp.where(slab_id < slabs - 1, below, -1),
        jnp.stack([slab_id, pool_id]).astype(jnp.int32),
    ])

    sent = gate(run_forward(plan, fwd_y, two_of(fwd_z.T), field), (meta,))
    pencils = lax.all_to_all(sent, "slab", split_axis=0, concat_axis=0, tiled=True)

    both = ("pool", "slab")
    firsts, packs, last = [], [], sent
    for group in plan.groups:
        lead, last, to_right, to_left = run_pack(plan, meta, esel, field, group, (last,))
        firsts.append(lax.ppermute(lead, "pool", [(0, 1)]))
        packs.append((
            last,
            lax.ppermute(to_right, both, [(i, i + 1) for i in range(slabs - 1)]),
            lax.ppermute(to_left, both, [(i + 1, i) for i in range(slabs - 1)]),
        ))

    partial = run_mix(plan, fwd_x, mode_local, pencils, (last,))
    halves = partial.reshape(2, ch, modes, plan.q)
    mine = lax.dynamic_index_in_dim(halves, ch_id, 0, keepdims=False)
    theirs = lax.dynamic_index_in_dim(halves, 1 - ch_id, 0, keepdims=False)
    mixed = run_sum(plan, mine, swapped(theirs, "ch", 0), (firsts[0],))

    back = run_back_x(plan, inv_x, mixed)
    owned = lax.all_to_all(back, "slab", split_axis=0, concat_axis=0, tiled=True)

    w_own, w_far, bias_rows = pointwise(plan, lin_local, bias_local, ch_id)
    lin = run_linear(plan, w_own, w_far, bias_rows, field, far_field, (back,))

    lead = 2 * plan.groups[0][1]
    rest = ch - lead
    hop = lax.ppermute(mixed[:lead], "pool", [(1, 0)])
    here = jnp.where(pool_id == 0, hop, mixed[ch - lead:])
    here = gate(here, (back,) + packs[0][1:])
    here = lax.all_gather(here, "slab", axis=0, tiled=False)
    seconds, last = [], lin
    for second, from_left, from_right in packs:
        last = run_assemble(plan, meta, second, from_left, from_right, (last, firsts[-1]))
        seconds.append(lax.ppermute(last, "pool", [(0, 1)]))
    gathered = [here, lax.ppermute(here[:, lead - rest:], "pool", [(1, 0)])]

    to_coarse = 0.5 * host_interp(plan.nz)
    gzp = (inv_z.T.astype(np.float32) @ to_coarse).astype(ml_dtypes.bfloat16)
    padded = np.pad(inv_x.reshape(slabs, planes, modes), ((1, 1), (0, 0), (0, 0)))
    gx3 = lax.dynamic_slice_in_dim(jnp.asarray(padded), slab_id, 3, 0)
    gx3 = gx3.reshape(3 * planes, modes)
    out = None
    for group, first_in, second, modes_in in zip(plan.groups, firsts, seconds, gathered):
        out = run_final(plan, meta, two_of(inv_z.T), two_of(gzp), gx3, inv_y, interp_tables(plan),
                        lin, first_in, second, modes_in, owned, group, out)
    return out


def plain_body(field, mode_local, lin_local, bias_local, own_row):
    bias_local = bias_local.astype(jnp.float32)
    own_ch, planes, y_cells, z_cells = field.shape
    modes = mode_local.shape[2]
    x_cells = planes * lax.axis_size("slab")
    block_count = own_row.shape[0]
    block_rows = y_cells // block_count
    slab_id = lax.axis_index("slab")
    is_coarse = lax.axis_index("pool") == 0
    fwd_x, inv_x = tables(x_cells, modes)
    fwd_y, inv_y = tables(y_cells, modes)
    fwd_z, inv_z = tables(z_cells, modes)
    pmat = interp_table(z_cells)
    z_table = jnp.where(is_coarse, pmat.T.astype(jnp.bfloat16), (0.5 * pmat).astype(jnp.bfloat16))
    block_ids = jnp.arange(block_count, dtype=jnp.int32)
    here_mask = (own_row == slab_id).astype(jnp.float32)[None, None, :, None]
    side_rows = [shifted(own_row, "slab", shift_by) for shift_by in (1, -1)]
    all_channels = lax.all_gather(field, "ch", axis=0, tiled=True)
    along_y = jnp.einsum("cxyz,my->cxmz", field, fwd_y, preferred_element_type=jnp.float32).astype(
        jnp.bfloat16
    )
    along_z = jnp.einsum(
        "cxmz,kz->cxmk", along_y, fwd_z, preferred_element_type=jnp.float32
    ).astype(jnp.bfloat16)
    along_z = along_z.reshape(own_ch, planes, modes * modes)
    pencils = lax.all_to_all(along_z, "slab", split_axis=2, concat_axis=1, tiled=True)
    coeffs = jnp.einsum("cxq,nx->cnq", pencils, fwd_x, preferred_element_type=jnp.float32).astype(
        jnp.bfloat16
    )
    partial_mix = jnp.einsum(
        "inq,ionq->onq", coeffs, mode_local, preferred_element_type=jnp.float32
    )
    mixed = lax.psum_scatter(
        partial_mix.astype(jnp.bfloat16), "ch", scatter_dimension=0, tiled=True
    )
    back_x = jnp.einsum("onq,xn->oxq", mixed, inv_x, preferred_element_type=jnp.float32).astype(
        jnp.bfloat16
    )
    back_x = lax.all_to_all(back_x, "slab", split_axis=1, concat_axis=2, tiled=True).reshape(
        own_ch, planes, modes, modes
    )
    back_z = jnp.einsum("cxmk,zk->cxmz", back_x, inv_z, preferred_element_type=jnp.float32).astype(
        jnp.bfloat16
    )
    spec = jnp.einsum("cxmz,ym->cxyz", back_z, inv_y, preferred_element_type=jnp.float32)
    flat_all = all_channels.reshape(all_channels.shape[0], planes * y_cells * z_cells)
    linear = jnp.einsum("io,ir->or", lin_local, flat_all, preferred_element_type=jnp.float32)
    linear = linear.reshape(own_ch, planes, y_cells, z_cells)
    anchor = jnp.where(is_coarse, field, spec.astype(jnp.bfloat16))
    payload = jnp.dot(anchor, z_table, preferred_element_type=jnp.float32).astype(jnp.bfloat16)
    partner = swapped(payload, "pool", 0)
    partner_blocks = partner.reshape(own_ch, planes, block_count, block_rows * z_cells)
    coupling = partner_blocks.astype(jnp.float32) * here_mask
    for shift_by, dest_row in ((1, side_rows[1]), (-1, side_rows[0])):
        sending = jnp.where(is_coarse, own_row == slab_id + shift_by, dest_row == slab_id).astype(
            jnp.int32
        )
        position = jnp.cumsum(sending) - 1
        slots = jnp.arange(HOP, dtype=jnp.int32)[:, None]
        select = (sending[None, :] == 1) & (position[None, :] == slots)
        packed = jnp.einsum(
            "hb,cxbr->cxhr",
            select.astype(jnp.bfloat16),
            partner_blocks,
            preferred_element_type=jnp.float32,
        ).astype(jnp.bfloat16)
        packed_ids = jnp.where(
            jnp.any(select, axis=1),
            jnp.sum(select.astype(jnp.int32) * block_ids[None, :], axis=1),
            -1,
        )
        arrived, arrived_ids = shifted((packed, packed_ids), "slab", shift_by)
        placing = (arrived_ids[:, None] == block_ids[None, :]).astype(jnp.bfloat16)
        coupling = coupling + jnp.einsum(
            "hb,cxhr->cxbr", placing, arrived, preferred_element_type=jnp.float32
        )
    total = (
        spec
        + linear
        + bias_local[:, None, None, None]
        + coupling.reshape(own_ch, planes, y_cells, z_cells)
    )
    return jax.nn.gelu(total, approximate=False).astype(jnp.bfloat16)


def body(fields, mode_weights, lin_weights, bias, source):
    args = (fields[0], mode_weights[0], lin_weights[0], bias[0], source[0])
    plan = Plan(args[0], args[1], args[4], lax.axis_size("slab"))
    if plan.fits():
        return fast_body(plan, *args)[None]
    return plain_body(*args)[None]


def solution(mesh):
    return jax.shard_map(
        body,
        mesh=mesh,
        in_specs=(
            P("pool", "ch", "slab", None, None),
            P("pool", "ch", None, None, "slab"),
            P("pool", None, "ch"),
            P("pool", "ch"),
            P("slab", None),
        ),
        out_specs=P("pool", "ch", "slab", None, None),
        check_vma=False,
    )
```
